32 devices in a mesh: cell: 16 (over z, y, x), gene: 2 (over core).
Axes of the slice: x: 2, y: 2, z: 4, core: 2. Of those that a mesh axis runs over, the one named last changes fastest.
Arguments:
- counts: int32 [2048, 32768], P('cell', 'gene'), may hold values from 0 to 3
- size_factor: int32 [2048], P('cell'), may hold values from 1200 to 2400
- gene_offset: float32 [32768], P('gene'), may hold values from -1.5 to 0.5
- factors: float32 [32, 2048], P(None, 'cell'), may hold values from -1.5 to 1.5
- loadings: float32 [32, 2, 16384], P(None, 'gene', 'cell'), may hold values from -1.5 to 1.5
Outputs:
- factors_next: float32 [32, 2048], P(None, 'cell')
- loadings_next: float32 [32, 2, 16384], P(None, 'gene', 'cell')
The draws below stay inside these ranges and needn't reach their ends.
All inputs are finite; a program needn't handle non-finite values.
Results may differ from the reference program's by a relative error of at most 0.0003.
Values sent between devices are 32-bit elements; how exact they have to be, the bound alone decides.
No kernel may reach another device: no remote copies, remote signals or barrier semaphores. Data moves between devices by JAX's collectives and lax.ppermute only.
A program may use at most 64 MiB of HBM per device.

```python
import math
import jax
import jax.numpy as jnp
from jax import lax

RANK = 32
GENES = 32768
ITERS = 2
FACTOR_STEPS = 4
CELLS = 2048
GROUPS = 2
SLAB = 16384


def set_ends(drawn, stream_key, smallest, top_value):
    index_at = [jax.random.randint(jax.random.fold_in(stream_key, axis), (), 0, length) for axis, length in enumerate(drawn.shape)]
    main_axis = drawn.shape.index(max(drawn.shape))
    neighbour = index_at[:main_axis] + [(index_at[main_axis] + 1) % drawn.shape[main_axis]] + index_at[main_axis + 1:]
    return drawn.at[tuple(index_at)].set(smallest).at[tuple(neighbour)].set(top_value)


def levels(own_key, extent, pieces, smallest, top_value):
    gain = 1.0
    for position, shards_of in pieces:
        steps = jax.random.uniform(jax.random.fold_in(jax.random.fold_in(own_key, 6), position), (shards_of,), jnp.float32, smallest / len(pieces), top_value / len(pieces))
        gain = gain * jnp.repeat(jnp.exp(steps), extent[position] // shards_of).reshape((-1,) + (1,) * (len(extent) - 1 - position))
    return gain


def noise(own_key, shape, scale, limit, cuts=(), kind=jnp.bfloat16):
    level = levels(own_key, shape, cuts, -0.22, 0.18) if cuts else 1.0
    values = jax.random.normal(own_key, shape, jnp.float32) * scale * level
    return jnp.minimum(jnp.maximum(values, -limit), limit).astype(kind)


def setup_inputs(seed: int = 0) -> dict:
    seeds = jax.random.split(jax.random.key(seed), 6)
    return {
        "counts": set_ends(jax.random.randint(seeds[0], (CELLS, GENES), 0, 4), jax.random.fold_in(seeds[0], 1), 0, 3).astype(jnp.int32),
        "size_factor": set_ends(jax.random.randint(seeds[1], (CELLS,), 1200, 2401), jax.random.fold_in(seeds[1], 1), 1200, 2400).astype(jnp.int32),
        "gene_offset": jnp.clip(-1.5 + 2.0 * jax.random.uniform(seeds[2], (GENES,), jnp.float32) ** levels(seeds[2], (GENES,), ((0, 2),), -0.2, 0.2), -1.5, 0.5),
        "factors": noise(seeds[3], (RANK, CELLS), 0.25, 1.5, ((1, 16),), jnp.float32),
        "loadings": noise(seeds[4], (RANK, GROUPS, SLAB), 0.25, 1.5, ((1, 2), (2, 16)), jnp.float32),
    }


HIGH = lax.Precision.HIGHEST

def shrink(values, level):
    kept = jnp.maximum(jnp.abs(values) - level, 0.0)
    return jnp.sign(values) * kept / 1.1

def reference(counts, size_factor, gene_offset, factors, loadings):
    block = math.gcd(CELLS, 1024)
    nblock = CELLS // block
    offset = jnp.log(size_factor.astype(jnp.float32) / 2000.0)
    current = factors
    whole = loadings.reshape(RANK, GENES)
    count_blocks = counts.reshape(nblock, block, GENES)
    offset_blocks = offset.reshape(nblock, block)
    eye = jnp.eye(RANK, dtype=jnp.float32)
    for step in range(ITERS):
        gram_u = jnp.dot(current, current.T, precision=HIGH)
        gram_v = jnp.dot(whole, whole.T, precision=HIGH)
        hess = gram_v + 0.1 * (jnp.trace(gram_v) / RANK) * eye
        chol = jnp.linalg.cholesky(hess)
        factor_blocks = current.reshape(RANK, nblock, block).transpose(1, 0, 2)

        def visit(carry, items):
            count_blk, offset_blk, factor_blk = items
            observed = count_blk.astype(jnp.float32)

            def resid_of(factor_now):
                eta = offset_blk[:, None] + gene_offset[None, :] + lax.dot_general(factor_now, whole, (((0,), (0,)), ((), ())), precision=HIGH)
                return jnp.exp(eta) - observed
            resid = resid_of(factor_blk)
            carry = carry + jnp.dot(factor_blk, resid, precision=HIGH)
            for turn in range(FACTOR_STEPS):
                if turn > 0:
                    resid = resid_of(factor_blk)
                grad_blk = lax.dot_general(whole, resid, (((1,), (1,)), ((), ())), precision=HIGH)
                factor_blk = factor_blk - 0.25 * jax.scipy.linalg.cho_solve((chol, True), grad_blk)
            return (carry, factor_blk)
        grad_v, new_blocks = lax.scan(visit, jnp.zeros((RANK, GENES), jnp.float32), (count_blocks, offset_blocks, factor_blocks))
        current = new_blocks.transpose(1, 0, 2).reshape(RANK, CELLS)
        rate = 0.5 * RANK / jnp.trace(gram_u)
        level = 0.1 * jnp.sqrt(jnp.trace(gram_v) / (RANK * GENES) + 1e-06)
        whole = shrink(whole - rate * grad_v, level)
    return (current, whole.reshape(RANK, GROUPS, SLAB))
```

```python
import functools
import math

import jax
import jax.numpy as jnp
from jax import lax
from jax.experimental import pallas as pl
from jax.experimental.pallas import tpu as pltpu
from jax.sharding import PartitionSpec as P

ITERS = 2
FACTOR_STEPS = 4
LOG2E = math.log2(math.e)
HIGH = lax.Precision.HIGHEST
F32 = jnp.float32
BF16 = jnp.bfloat16
VMEM_LIMIT = 14 * 1024 * 1024
NT = (((1,), (1,)), ((), ()))


def split(x, n):
    parts = []
    for i in range(n):
        part = x.astype(BF16)
        parts.append(part)
        if i < n - 1:
            x = x - part.astype(F32)
    return parts


def dot(a, b):
    return jnp.dot(a, b, preferred_element_type=F32)


def dot_nt(a, b):
    return lax.dot_general(a, b, NT, preferred_element_type=F32)


def factor_operand(u, size_row):
    rank, cells = u.shape
    u1, u2 = [p.astype(F32) for p in split(u * LOG2E, 2)]
    offsets = [p.astype(F32) for p in split(jnp.log(size_row.astype(F32) / 2000.0) * LOG2E, 3)]
    row = lax.broadcasted_iota(jnp.int32, (128 - 3 * rank, cells), 0)
    extra = jnp.where(row < 3, 1.0, 0.0)
    for i, o in enumerate(offsets):
        extra = jnp.where(row == 3 + i, o, extra)
    one = jnp.concatenate([u1, u1, u2, extra], 0)
    none = jnp.zeros_like(one)
    return jnp.concatenate([jnp.concatenate([one, none], 1), jnp.concatenate([none, one], 1)], 0).astype(BF16)


def gene_operand(v1, v2, gene_row):
    rank, genes = v1.shape
    row = lax.broadcasted_iota(jnp.int32, (128 - 3 * rank, genes), 0)
    extra = jnp.where(row < 6, 1.0, 0.0)
    for i, g in enumerate(split(gene_row * LOG2E, 3)):
        extra = jnp.where(row == i, g.astype(F32), extra)
    return jnp.concatenate([v1, v2, v1, extra.astype(BF16)], 0)


def fold(acc, rank):
    return acc[:rank] + acc[rank:]


def owner_of(owners, block):
    if owners[1] is None:
        return owners[0][block]
    even, odd = owners[0][block], owners[1][block]
    mask = jnp.where(lax.axis_index("gene") % 2 == 1, odd, even)
    return lax.axis_index("cell") ^ mask


def columns_of(owners, block, width):
    start = owner_of(owners, block) * width
    return pl.ds(start if isinstance(start, int) else pl.multiple_of(start, 128), width)


def counts_kernel(owners, counts, u, uc, cb, landed, sems):
    rank = u.shape[0]
    blocks, _, width = landed.shape
    copies = [
        pltpu.make_async_copy(counts.at[:, columns_of(owners, i, width)], landed.at[i], sems.at[i]) for i in range(blocks)
    ]
    for copy in copies:
        copy.start()
    left = jnp.concatenate(split(u[...], 2), 0)
    for i, copy in enumerate(copies):
        copy.wait()
        c = landed[i].astype(F32).astype(BF16)
        cb[:, i * width : (i + 1) * width] = c
        uc[i * rank : (i + 1) * rank, :] = fold(dot(left, c), rank)


def first_counts(owners, counts, u, width, room):
    rank, cells = u.shape
    blocks = len(owners[0])
    vmem = pl.BlockSpec(memory_space=pltpu.VMEM)
    return pl.pallas_call(
        functools.partial(counts_kernel, owners),
        in_specs=[pl.BlockSpec(memory_space=pltpu.HBM), vmem],
        out_specs=[vmem] * 2,
        out_shape=[
            jax.ShapeDtypeStruct((blocks * rank, width), F32),
            jax.ShapeDtypeStruct((cells, blocks * width), BF16),
        ],
        scratch_shapes=[pltpu.VMEM((blocks, cells, width), jnp.int32), pltpu.SemaphoreType.DMA((blocks,))],
        compiler_params=pltpu.CompilerParams(vmem_limit_bytes=room * 1024 * 1024),
        cost_estimate=cost(blocks * width, cells, 512),
        name="first_counts",
    )(counts, u)


def message_of(u, size_row, v):
    row = lax.broadcasted_iota(jnp.int32, (8, u.shape[1]), 0)
    return jnp.concatenate([u, jnp.where(row == 0, size_row.astype(F32), jnp.sum(v * v))], 0)


def entry_kernel(size_row, u, raw, v_out, message):
    v = raw[...].reshape(v_out.shape)
    v_out[...] = v
    message[...] = message_of(u[...], size_row[...], v)


def entry(size_row, u, raw):
    rank, cells = u.shape
    return pl.pallas_call(
        entry_kernel,
        out_shape=[
            jax.ShapeDtypeStruct((rank, raw.shape[2]), F32),
            jax.ShapeDtypeStruct((rank + 8, cells), F32),
        ],
        compiler_params=params(),
        name="entry",
    )(size_row, u, raw)


def pairs(e1, e2):
    cells = e1.shape[1] // 2
    top = jnp.concatenate([e1[:, :cells], e2[:, :cells]], 1)
    bottom = jnp.concatenate([e1[:, cells:], e2[:, cells:]], 1)
    return jnp.concatenate([top, bottom], 0)


def start_kernel(last, owners, gene_row, size_row, u_ref, v, cb, *refs):
    if last:
        gu_in, rest_in, w, st, packed, vc, weights, eb = refs
    else:
        w, st, gu_out, rest_out, weights, eb = refs
    u = u_ref[...]
    rank, cells = u.shape
    blocks, width = v.shape[0] // rank, v.shape[1]
    groups = blocks // 2
    weights[...] = factor_operand(u, size_row[...])
    gu = gu_in[...] if last else jnp.zeros((2 * rank, 2 * cells), F32)
    rest = rest_in[...] if last else jnp.zeros((2 * rank, cells + 2 * rank), F32)

    def prepare(i):
        for j in range(2):
            block = 2 * i + j
            v1, v2 = split(v[block * rank : (block + 1) * rank, :], 2)
            st[:, block * width : (block + 1) * width] = jnp.concatenate([v1, v2], 0)
            genes = gene_row[:, columns_of(owners, block, width)]
            w[i * width : (i + 1) * width, 128 * j : 128 * (j + 1)] = gene_operand(v1, v2, genes).T

    def front(i):
        eb[i % 2] = dot(w[i * width : (i + 1) * width, :], weights[...])

    for i in range(groups + 2):
        if i < groups:
            prepare(i)
        if 1 <= i <= groups:
            front(i - 1)
        if i >= 2:
            at = (i - 2) * 2 * width
            s = st[:, at : at + 2 * width]
            gu = gu + dot(s, pairs(*split(jnp.exp2(eb[i % 2]), 2)))
            rest = rest + dot_nt(s, jnp.concatenate([cb[:, at : at + 2 * width], s], 0))
    if not last:
        gu_out[...] = gu
        rest_out[...] = rest
        return
    gu, rest = fold(gu, rank), fold(rest, rank)
    vc[...] = rest[:, :cells]
    packed[:, :cells] = gu[:, :cells] + gu[:, cells:] - rest[:, :cells]
    gram = rest[:, cells : cells + rank] + rest[:, cells + rank :]
    packed[:, cells:] = jnp.concatenate([gram, jnp.zeros((rank, packed.shape[1] - cells - rank), F32)], 1)


def start_part(owners, gene_row, size_row, u, v, cb, sums=()):
    rank, cells = u.shape
    width = v.shape[1]
    genes = v.shape[0] // rank * width
    last = bool(sums)
    vmem = pl.BlockSpec(memory_space=pltpu.VMEM)
    shapes = ((rank, cells + 128), (rank, cells)) if last else ((2 * rank, 2 * cells), (2 * rank, cells + 2 * rank))
    return pl.pallas_call(
        functools.partial(start_kernel, last, owners),
        in_specs=[vmem] * (5 + len(sums)),
        out_specs=[vmem] * 4,
        out_shape=[
            jax.ShapeDtypeStruct((genes // 2, 256), BF16),
            jax.ShapeDtypeStruct((2 * rank, genes), BF16),
        ]
        + [jax.ShapeDtypeStruct(shape, F32) for shape in shapes],
        scratch_shapes=[
            pltpu.VMEM((256, 2 * cells), BF16),
            pltpu.VMEM((2, width, 2 * cells), F32),
        ],
        compiler_params=params(),
        cost_estimate=cost(genes, cells, 1024),
        name="start_part",
    )(gene_row, size_row, u, v, cb, *sums)


def own_kernel(v_ref, gene_row, u_all, grad, traces, eb):
    v = v_ref[...]
    rank, genes = v.shape
    rows = rank + 8
    blocks = u_all.shape[0] // rows
    v1, v2 = split(v, 2)
    place = lax.axis_index("cell") * genes
    own = slice(None) if gene_row.shape[1] == genes else pl.ds(pl.multiple_of(place, 128), genes)
    op = gene_operand(v1, v2, gene_row[:, own]).T
    w = jnp.concatenate([op[: genes // 2], op[genes // 2 :]], 1)
    g = jnp.zeros((2 * rank, genes), F32)
    trace_u = jnp.zeros((1, 1), F32)
    trace_v = jnp.zeros((1, 1), F32)

    def front(i):
        u = u_all[i * rows : i * rows + rank, :]
        eb[i % 2] = dot(w, factor_operand(u, u_all[i * rows + rank : i * rows + rank + 1, :]))

    front(0)
    for i in range(blocks):
        if i + 1 < blocks:
            front(i + 1)
        u = u_all[i * rows : i * rows + rank, :]
        left = jnp.concatenate(split(u, 2), 0)
        g = g + dot_nt(jnp.concatenate([left, left], 1), pairs(*split(jnp.exp2(eb[i % 2]), 2)))
        trace_u = trace_u + jnp.sum(u * u)
        trace_v = trace_v + u_all[i * rows + rank + 1 : i * rows + rank + 2, :1]
    grad[...] = fold(g, rank)
    row = lax.broadcasted_iota(jnp.int32, (8, 128), 0)
    traces[...] = jnp.where(row == 0, trace_u, trace_v)


def own_gradient(v, gene_row, u_all):
    rank, genes = v.shape
    return pl.pallas_call(
        own_kernel,
        out_shape=[jax.ShapeDtypeStruct(v.shape, F32), jax.ShapeDtypeStruct((8, 128), F32)],
        scratch_shapes=[pltpu.VMEM((2, genes // 2, 256), F32)],
        compiler_params=params(),
        cost_estimate=cost(genes, u_all.shape[0] // (rank + 8) * 128, 1024),
        name="own_gradient",
    )(v, gene_row, u_all)


def loadings_kernel(values, v, grad, kept, got, traces, mine, other, out):
    rank = v.shape[0]
    rate = 0.5 * rank / traces[0:1, 0:1]
    level = 0.1 * jnp.sqrt((mine[1:2, 0:1] + other[1:2, 0:1]) / values + 1e-06)
    moved = v[...] - rate * (grad[...] - (kept[...] + got[...]))
    less = jnp.maximum(jnp.abs(moved) - level, 0.0) / 1.1
    out[...] = jnp.where(moved < 0.0, -less, less).reshape(out.shape)


def next_loadings(values, shape, v, grad, kept, got, traces, mine, other):
    return pl.pallas_call(
        functools.partial(loadings_kernel, values),
        out_shape=jax.ShapeDtypeStruct(shape, F32),
        compiler_params=params(),
        name="next_loadings",
    )(v, grad, kept, got, traces, mine, other)


def invert(gram):
    rank = gram.shape[0]
    row = lax.broadcasted_iota(jnp.int32, (rank, rank), 0)
    col = lax.broadcasted_iota(jnp.int32, (rank, rank), 1)
    lane = lax.broadcasted_iota(jnp.int32, (1, rank), 1)
    diag = row == col
    trace = jnp.sum(jnp.where(diag, gram, 0.0))
    a = gram + jnp.where(diag, 0.1 * (trace / rank), 0.0)
    for k in range(0, rank, 2):
        row0, row1 = a[k : k + 1, :], a[k + 1 : k + 2, :]
        col0, col1 = a[:, k : k + 1], a[:, k + 1 : k + 2]
        p, q, r = a[k : k + 1, k : k + 1], a[k : k + 1, k + 1 : k + 2], a[k + 1 : k + 2, k + 1 : k + 2]
        scale = 1.0 / (p * r - q * q)
        p, q, r = r * scale, -q * scale, p * scale
        new0, new1 = p * row0 + q * row1, q * row0 + r * row1
        rest = a - (col0 * new0 + col1 * new1)
        rest = jnp.where(col == k, col0 * p + col1 * q, jnp.where(col == k + 1, col0 * q + col1 * r, rest))
        new0 = jnp.where(lane == k, -p, jnp.where(lane == k + 1, -q, new0))
        new1 = jnp.where(lane == k, -q, jnp.where(lane == k + 1, -r, new1))
        a = jnp.where(row == k, new0, jnp.where(row == k + 1, new1, rest))
    return -a


def inverse_kernel(cells, mine, other, hinv):
    hinv[...] = invert((mine[...] + other[...])[:, cells : cells + mine.shape[0]])


def inverse_of(cells, mine, other):
    rank = mine.shape[0]
    return pl.pallas_call(
        functools.partial(inverse_kernel, cells),
        out_shape=jax.ShapeDtypeStruct((rank, rank), F32),
        compiler_params=params(),
        cost_estimate=cost(16384, 128, 1024),
        name="inverse",
    )(mine, other)


def next_kernel(size_row, u, mine, other, hinv, vc, w1, w2, st1, st2, grad, u_out, weights, eb):
    rank, cells = u.shape
    total = mine[:, :cells] + other[:, :cells]
    now = u[...] - 0.25 * jnp.dot(hinv[...], total, precision=HIGH, preferred_element_type=F32)
    u_out[...] = now
    weights[...] = factor_operand(now, size_row[...])
    half = eb.shape[1]
    work = [(w, st, at) for w, st in ((w1, st1), (w2, st2)) for at in range(0, st.shape[1], 2 * half)]

    def front(i):
        w, _, at = work[i]
        eb[i % 2] = dot(w[at // 2 : at // 2 + half, :], weights[...])

    acc = jnp.zeros((2 * rank, 2 * cells), F32)
    front(0)
    for i, (_, st, at) in enumerate(work):
        if i + 1 < len(work):
            front(i + 1)
        acc = acc + dot(st[:, at : at + 2 * half], pairs(*split(jnp.exp2(eb[i % 2]), 2)))
    g = fold(acc, rank)
    grad[...] = g[:, :cells] + g[:, cells:] - vc[...]


def next_turn(width, size_row, u, mine, other, hinv, vc, w1, w2, st1, st2):
    rank, cells = u.shape
    return pl.pallas_call(
        next_kernel,
        out_shape=[jax.ShapeDtypeStruct((rank, cells), F32)] * 2,
        scratch_shapes=[
            pltpu.VMEM((256, 2 * cells), BF16),
            pltpu.VMEM((2, width, 2 * cells), F32),
        ],
        compiler_params=params(),
        cost_estimate=cost(2 * st1.shape[1], cells, 1024),
        name="next_turn",
    )(size_row, u, mine, other, hinv, vc, w1, w2, st1, st2)


def last_kernel(u, mine, other, hinv, u_out):
    total = mine[...] + other[...]
    u_out[...] = u[...] - 0.25 * jnp.dot(hinv[...], total, precision=HIGH, preferred_element_type=F32)


def last_update(u, mine, other, hinv):
    return pl.pallas_call(
        last_kernel,
        out_shape=jax.ShapeDtypeStruct(u.shape, F32),
        compiler_params=params(),
        name="last_update",
    )(u, mine, other, hinv)


def step_kernel(width, u, mine, other, hinv, size_row, v, cb0, cb1, u_out, message, uc0, uc1):
    rank = u.shape[0]
    total = mine[...] + other[...]
    now = u[...] - 0.25 * jnp.dot(hinv[...], total, precision=HIGH, preferred_element_type=F32)
    u_out[...] = now
    message[...] = message_of(now, size_row[...], v[...])
    left = jnp.concatenate(split(now, 2), 0)
    for cb, uc in ((cb1, uc1), (cb0, uc0)):
        for block in range(cb.shape[1] // width):
            c = cb[:, block * width : (block + 1) * width]
            uc[block * rank : (block + 1) * rank, :] = fold(dot(left, c), rank)


def step_update(width, u, mine, other, hinv, size_row, v, cb0, cb1):
    rank, cells = u.shape
    sums = jax.ShapeDtypeStruct((cb0.shape[1] // width * rank, width), F32)
    return pl.pallas_call(
        functools.partial(step_kernel, width),
        out_shape=[
            jax.ShapeDtypeStruct((rank, cells), F32),
            jax.ShapeDtypeStruct((rank + 8, cells), F32),
            sums,
            sums,
        ],
        compiler_params=params(),
        cost_estimate=cost(2 * cb0.shape[1], cells, 256),
        name="step_update",
    )(u, mine, other, hinv, size_row, v, cb0, cb1)


def params():
    return pltpu.CompilerParams(vmem_limit_bytes=VMEM_LIMIT)


def cost(genes, cells, depth):
    return pl.CostEstimate(flops=genes * cells * depth // 16, bytes_accessed=genes * cells // 4, transcendentals=genes * cells // 16)


def solution(mesh):
    n_cell = mesh.shape["cell"]
    n_gene = mesh.shape["gene"]
    bits = [1 << b for b in range(n_cell.bit_length() - 1)][::-1]
    far, near = bits[:-2], bits[-2:]
    orders = far + near, far[::-1] + near[::-1]
    near_first = near + far, near[::-1] + far[::-1]
    rounds = len(bits)

    def swap(x, step, order=orders):
        perm = [(i * n_gene + g, (i ^ order[g % 2][step]) * n_gene + g) for i in range(n_cell) for g in range(n_gene)]
        return lax.ppermute(x, ("cell", "gene"), perm)

    def sum_gene(x):
        for step in range(n_gene.bit_length() - 2, -1, -1):
            got = lax.ppermute(x, "gene", [(g, g ^ (1 << step)) for g in range(n_gene)])
            if step:
                x = x + got
        return x, got

    def masks(order):
        out = [0]
        for bit in order:
            out = out + [i | bit for i in out]
        return out

    def on_device(counts, size_factor, gene_offset, factors, loadings):
        rank, cells = factors.shape
        width = loadings.shape[2]
        slab = width * n_cell
        size_row = size_factor.reshape(1, -1)
        gene_row = gene_offset.reshape(1, -1)
        direct = width % 256 == 0
        block = width if direct else slab // 4
        if direct:
            half = n_cell // 2
            even, odd = [masks(o) for o in orders]
            owners = (even[:half], odd[:half]), (even[half:], odd[half:])
            own_row = gene_row
        else:
            owners = ([0, 1], None), ([2, 3], None)
            own_row = lax.dynamic_slice_in_dim(gene_row, lax.axis_index("cell") * width, width, 1)

        def double(x, step, order=orders):
            return jnp.concatenate([x, swap(x, step, order)], 0)

        def halve(x, step):
            rows = x.shape[0] // 2
            return x[:rows], swap(x[rows:], step)

        def together(*xs):
            return lax.optimization_barrier(xs)

        def gather_plain(x):
            x = lax.all_gather(x, "cell", axis=1, tiled=True)
            x = x.reshape(rank, 2, 2, block).transpose(1, 2, 0, 3).reshape(2, 2 * rank, block)
            return x[0], x[1]

        def scatter_plain(x0, x1):
            x = jnp.stack([x0, x1]).reshape(4, rank, block).transpose(1, 0, 2).reshape(rank, slab)
            x = lax.psum_scatter(x, "cell", scatter_dimension=1, tiled=True)
            return x, jnp.zeros_like(x)

        def first_exchange(v, message):
            u_now, v, message = together(u, v, message)
            b, g = double(v, 0), double(message, 0, near_first)
            uc1, cb1 = first_counts(owners[1], counts, u_now, block, 57)
            uc1, g, b = together(uc1, g, b)
            got = swap(uc1, rounds - 1)
            a, cb0 = first_counts(owners[0], counts, u, block, 50)
            for step in range(1, len(far)):
                b = double(b, step)
            for step in range(1, len(near)):
                g = double(g, step, near_first)
            a, got, b, g = together(a, got, b, g)
            for step in range(len(far), rounds - 1):
                a, got = halve(a + got, rounds - 2 - step + len(far))
                b = double(b, step)
                a, got, b = together(a, got, b)
            for step in range(len(near), rounds):
                g = double(g, step, near_first)
            grad_v, traces = own_gradient(v, own_row, g)
            traces, *of_gene = traces, *sum_gene(traces)
            a, got, b, grad_v, traces, *of_gene = together(a, got, b, grad_v, traces, *of_gene)
            p1 = swap(b, rounds - 1)
            begun = start_part(owners[0], gene_row, size_row, u, b, cb0)
            for step in range(rounds - 1 - len(near), -1, -1):
                a, got = halve(a + got, step)
                if step:
                    a, got, *begun = together(a, got, *begun)
            return (cb0, cb1), p1, begun, grad_v, (traces, *of_gene), a, got

        def own_of(v, message):
            g = message
            for step in range(rounds):
                g = double(g, step)
            return own_gradient(v, own_row, g)

        def plain_exchange(v, message, uc0, uc1):
            g = lax.all_gather(message, "cell", axis=0, tiled=True)
            return *own_gradient(v, own_row, g), *scatter_plain(uc0, uc1)

        u = factors
        v, message = entry(size_row, u, loadings)
        for step in range(ITERS):
            if not direct:
                if step == 0:
                    uc1, cb1 = first_counts(owners[1], counts, u, block, 14)
                    uc0, cb0 = first_counts(owners[0], counts, u, block, 14)
                p0, p1 = gather_plain(v)
                grad_v, traces, kept, got = plain_exchange(v, message, uc0, uc1)
                traces = traces, *sum_gene(traces)
                begun = start_part(owners[0], gene_row, size_row, u, p0, cb0)
            elif step == 0:
                (cb0, cb1), p1, begun, grad_v, traces, kept, got = first_exchange(v, message)
            else:
                begun = start_part(owners[0], gene_row, size_row, u, p0, cb0)
                p1, *begun = together(p1, *begun)
                uc1, p1 = together(uc1, p1)
                kept, got = uc0, swap(uc1, rounds - 1)
                grad_v, traces = own_of(v, message)
                traces = traces, *sum_gene(traces)

            def loadings_now(kept, got):
                shape = v.shape if step < ITERS - 1 else (rank, 1, width)
                return next_loadings(rank * slab * n_gene, shape, v, grad_v, kept, got, *traces)

            if not direct:
                v = loadings_now(kept, got)
                beside = lambda x, turn: x
            elif step < ITERS - 1:
                v = loadings_now(kept, got)
                state = {"held": v}

                def beside(x, turn):
                    if turn < rounds - 1:
                        x, got = together(x, swap(state["held"], turn))
                        state["held"] = jnp.concatenate([state["held"], got], 0)
                    if turn == rounds - 2:
                        state["last"] = swap(state["held"], rounds - 1)
                    return x
            else:
                state = {"kept": kept, "got": got, "step": rounds - 2}

                def beside(x, turn):
                    if turn == 2 or turn >= FACTOR_STEPS:
                        x, kept, got = together(x, state["kept"], state["got"])
                        state["kept"], state["got"] = halve(kept + got, state["step"])
                        state["step"] -= 1
                    return x

            w1, st1, *sums = begun
            w2, st2, packed, vc = start_part(owners[1], gene_row, size_row, u, p1, cb1, sums)
            mine, other = sum_gene(packed)
            mine = beside(mine, 0)
            hinv = beside(inverse_of(cells, mine, other), 1)
            for turn in range(2, FACTOR_STEPS + 1):
                mine, u = next_turn(block, size_row, u, mine, other, hinv, vc, w1, w2, st1, st2)
                mine, other = sum_gene(mine)
                if turn < FACTOR_STEPS:
                    mine = beside(mine, turn)
            if step < ITERS - 1:
                u, message, uc0, uc1 = step_update(block, u, mine, other, hinv, size_row, v, cb0, cb1)
            else:
                u = last_update(u, mine, other, hinv)
            if direct and step == ITERS - 1:
                (grad_v, mine), turn = together(grad_v, mine), FACTOR_STEPS
                while state["step"] >= 0:
                    mine = beside(mine, turn)
            elif direct:
                for turn in range(FACTOR_STEPS, rounds - 1):
                    mine = beside(mine, turn)
            if direct and step < ITERS - 1:
                p0, p1 = state["held"], state["last"]
            elif direct:
                v = loadings_now(state["kept"], state["got"])
        return (u, v.reshape(rank, 1, width))

    return jax.shard_map(
        on_device,
        mesh=mesh,
        in_specs=(
            P("cell", "gene"),
            P("cell"),
            P("gene"),
            P(None, "cell"),
            P(None, "gene", "cell"),
        ),
        out_specs=(P(None, "cell"), P(None, "gene", "cell")),
        check_vma=False,
    )
```

```python
import functools
import math

import jax
import jax.numpy as jnp
from jax import lax
from jax.experimental import pallas as pl
from jax.experimental.pallas import tpu as pltpu
from jax.sharding import PartitionSpec as P

ITERS = 2
FACTOR_STEPS = 4
LOG2E = math.log2(math.e)
HIGH = lax.Precision.HIGHEST
F32 = jnp.float32
BF16 = jnp.bfloat16
VMEM_LIMIT = 14 * 1024 * 1024
NT = (((1,), (1,)), ((), ()))


def split(x, n):
    parts = []
    for i in range(n):
        part = x.astype(BF16)
        parts.append(part)
        if i < n - 1:
            x = x - part.astype(F32)
    return parts


def dot(a, b):
    return jnp.dot(a, b, preferred_element_type=F32)


def dot_nt(a, b):
    return lax.dot_general(a, b, NT, preferred_element_type=F32)


def factor_operand(u, size_row):
    rank, cells = u.shape
    u1, u2 = [p.astype(F32) for p in split(u * LOG2E, 2)]
    offsets = [p.astype(F32) for p in split(jnp.log(size_row.astype(F32) / 2000.0) * LOG2E, 3)]
    row = lax.broadcasted_iota(jnp.int32, (128 - 3 * rank, cells), 0)
    extra = jnp.where(row < 3, 1.0, 0.0)
    for i, o in enumerate(offsets):
        extra = jnp.where(row == 3 + i, o, extra)
    one = jnp.concatenate([u1, u1, u2, extra], 0)
    none = jnp.zeros_like(one)
    return jnp.concatenate([jnp.concatenate([one, none], 1), jnp.concatenate([none, one], 1)], 0).astype(BF16)


def gene_operand(v1, v2, gene_row):
    rank, genes = v1.shape
    row = lax.broadcasted_iota(jnp.int32, (128 - 3 * rank, genes), 0)
    extra = jnp.where(row < 6, 1.0, 0.0)
    for i, g in enumerate(split(gene_row * LOG2E, 3)):
        extra = jnp.where(row == i, g.astype(F32), extra)
    return jnp.concatenate([v1, v2, v1, extra.astype(BF16)], 0)


def fold(acc, rank):
    return acc[:rank] + acc[rank:]


def owner_of(owners, block):
    if owners[1] is None:
        return owners[0][block]
    even, odd = owners[0][block], owners[1][block]
    mask = jnp.where(lax.axis_index("gene") % 2 == 1, odd, even)
    return lax.axis_index("cell") ^ mask


def columns_of(owners, block, width):
    start = owner_of(owners, block) * width
    return pl.ds(start if isinstance(start, int) else pl.multiple_of(start, 128), width)


def counts_kernel(owners, counts, u, uc, cb, landed, sems):
    rank = u.shape[0]
    blocks, _, width = landed.shape
    copies = [
        pltpu.make_async_copy(counts.at[:, columns_of(owners, i, width)], landed.at[i], sems.at[i]) for i in range(blocks)
    ]
    for copy in copies:
        copy.start()
    left = jnp.concatenate(split(u[...], 2), 0)
    for i, copy in enumerate(copies):
        copy.wait()
        c = landed[i].astype(F32).astype(BF16)
        cb[:, i * width : (i + 1) * width] = c
        uc[i * rank : (i + 1) * rank, :] = fold(dot(left, c), rank)


def first_counts(owners, counts, u, width, room=14):
    rank, cells = u.shape
    blocks = len(owners[0])
    vmem = pl.BlockSpec(memory_space=pltpu.VMEM)
    return pl.pallas_call(
        functools.partial(counts_kernel, owners),
        in_specs=[pl.BlockSpec(memory_space=pltpu.HBM), vmem],
        out_specs=[vmem] * 2,
        out_shape=[
            jax.ShapeDtypeStruct((blocks * rank, width), F32),
            jax.ShapeDtypeStruct((cells, blocks * width), BF16),
        ],
        scratch_shapes=[pltpu.VMEM((blocks, cells, width), jnp.int32), pltpu.SemaphoreType.DMA((blocks,))],
        compiler_params=pltpu.CompilerParams(vmem_limit_bytes=room * 1024 * 1024),
        cost_estimate=cost(blocks * width, cells, 512),
        name="first_counts",
    )(counts, u)


def message_of(u, size_row, v):
    row = lax.broadcasted_iota(jnp.int32, (8, u.shape[1]), 0)
    return jnp.concatenate([u, jnp.where(row == 0, size_row.astype(F32), jnp.sum(v * v))], 0)


def entry_kernel(size_row, u, raw, v_out, message):
    v = raw[...].reshape(v_out.shape)
    v_out[...] = v
    message[...] = message_of(u[...], size_row[...], v)


def entry(size_row, u, raw):
    rank, cells = u.shape
    return pl.pallas_call(
        entry_kernel,
        out_shape=[
            jax.ShapeDtypeStruct((rank, raw.shape[2]), F32),
            jax.ShapeDtypeStruct((rank + 8, cells), F32),
        ],
        compiler_params=params(),
        name="entry",
    )(size_row, u, raw)


def pairs(e1, e2):
    cells = e1.shape[1] // 2
    top = jnp.concatenate([e1[:, :cells], e2[:, :cells]], 1)
    bottom = jnp.concatenate([e1[:, cells:], e2[:, cells:]], 1)
    return jnp.concatenate([top, bottom], 0)


def start_kernel(last, owners, gene_row, size_row, u_ref, v, cb, *refs):
    if last:
        gu_in, rest_in, w, st, packed, vc, weights, eb = refs
    else:
        w, st, gu_out, rest_out, weights, eb = refs
    u = u_ref[...]
    rank, cells = u.shape
    blocks, width = v.shape[0] // rank, v.shape[1]
    groups = blocks // 2
    weights[...] = factor_operand(u, size_row[...])
    gu = gu_in[...] if last else jnp.zeros((2 * rank, 2 * cells), F32)
    rest = rest_in[...] if last else jnp.zeros((2 * rank, cells + 2 * rank), F32)

    def prepare(i):
        for j in range(2):
            block = 2 * i + j
            v1, v2 = split(v[block * rank : (block + 1) * rank, :], 2)
            st[:, block * width : (block + 1) * width] = jnp.concatenate([v1, v2], 0)
            genes = gene_row[:, columns_of(owners, block, width)]
            w[i * width : (i + 1) * width, 128 * j : 128 * (j + 1)] = gene_operand(v1, v2, genes).T

    def front(i):
        eb[i % 2] = dot(w[i * width : (i + 1) * width, :], weights[...])

    for i in range(groups + 2):
        if i < groups:
            prepare(i)
        if 1 <= i <= groups:
            front(i - 1)
        if i >= 2:
            at = (i - 2) * 2 * width
            s = st[:, at : at + 2 * width]
            gu = gu + dot(s, pairs(*split(jnp.exp2(eb[i % 2]), 2)))
            rest = rest + dot_nt(s, jnp.concatenate([cb[:, at : at + 2 * width], s], 0))
    if not last:
        gu_out[...] = gu
        rest_out[...] = rest
        return
    gu, rest = fold(gu, rank), fold(rest, rank)
    vc[...] = rest[:, :cells]
    packed[:, :cells] = gu[:, :cells] + gu[:, cells:] - rest[:, :cells]
    gram = rest[:, cells : cells + rank] + rest[:, cells + rank :]
    packed[:, cells:] = jnp.concatenate([gram, jnp.zeros((rank, packed.shape[1] - cells - rank), F32)], 1)


def start_part(owners, gene_row, size_row, u, v, cb, sums=()):
    rank, cells = u.shape
    width = v.shape[1]
    genes = v.shape[0] // rank * width
    last = bool(sums)
    vmem = pl.BlockSpec(memory_space=pltpu.VMEM)
    shapes = ((rank, cells + 128), (rank, cells)) if last else ((2 * rank, 2 * cells), (2 * rank, cells + 2 * rank))
    return pl.pallas_call(
        functools.partial(start_kernel, last, owners),
        in_specs=[vmem] * (5 + len(sums)),
        out_specs=[vmem] * 4,
        out_shape=[
            jax.ShapeDtypeStruct((genes // 2, 256), BF16),
            jax.ShapeDtypeStruct((2 * rank, genes), BF16),
        ]
        + [jax.ShapeDtypeStruct(shape, F32) for shape in shapes],
        scratch_shapes=[
            pltpu.VMEM((256, 2 * cells), BF16),
            pltpu.VMEM((2, width, 2 * cells), F32),
        ],
        compiler_params=params(),
        cost_estimate=cost(genes, cells, 1024),
        name="start_part",
    )(gene_row, size_row, u, v, cb, *sums)


def own_kernel(v_ref, gene_row, u_all, grad, traces, eb):
    v = v_ref[...]
    rank, genes = v.shape
    rows = rank + 8
    blocks = u_all.shape[0] // rows
    v1, v2 = split(v, 2)
    place = lax.axis_index("cell") * genes
    own = slice(None) if gene_row.shape[1] == genes else pl.ds(pl.multiple_of(place, 128), genes)
    op = gene_operand(v1, v2, gene_row[:, own]).T
    w = jnp.concatenate([op[: genes // 2], op[genes // 2 :]], 1)
    g = jnp.zeros((2 * rank, genes), F32)
    trace_u = jnp.zeros((1, 1), F32)
    trace_v = jnp.zeros((1, 1), F32)

    def front(i):
        u = u_all[i * rows : i * rows + rank, :]
        eb[i % 2] = dot(w, factor_operand(u, u_all[i * rows + rank : i * rows + rank + 1, :]))

    front(0)
    for i in range(blocks):
        if i + 1 < blocks:
            front(i + 1)
        u = u_all[i * rows : i * rows + rank, :]
        left = jnp.concatenate(split(u, 2), 0)
        g = g + dot_nt(jnp.concatenate([left, left], 1), pairs(*split(jnp.exp2(eb[i % 2]), 2)))
        trace_u = trace_u + jnp.sum(u * u)
        trace_v = trace_v + u_all[i * rows + rank + 1 : i * rows + rank + 2, :1]
    grad[...] = fold(g, rank)
    row = lax.broadcasted_iota(jnp.int32, (8, 128), 0)
    traces[...] = jnp.where(row == 0, trace_u, trace_v)


def own_gradient(v, gene_row, u_all):
    rank, genes = v.shape
    return pl.pallas_call(
        own_kernel,
        out_shape=[jax.ShapeDtypeStruct(v.shape, F32), jax.ShapeDtypeStruct((8, 128), F32)],
        scratch_shapes=[pltpu.VMEM((2, genes // 2, 256), F32)],
        compiler_params=params(),
        cost_estimate=cost(genes, u_all.shape[0] // (rank + 8) * 128, 1024),
        name="own_gradient",
    )(v, gene_row, u_all)


def loadings_kernel(values, v, grad, kept, got, traces, mine, other, out):
    rank = v.shape[0]
    rate = 0.5 * rank / traces[0:1, 0:1]
    level = 0.1 * jnp.sqrt((mine[1:2, 0:1] + other[1:2, 0:1]) / values + 1e-06)
    moved = v[...] - rate * (grad[...] - (kept[...] + got[...]))
    less = jnp.maximum(jnp.abs(moved) - level, 0.0) / 1.1
    out[...] = jnp.where(moved < 0.0, -less, less).reshape(out.shape)


def next_loadings(values, shape, v, grad, kept, got, traces, mine, other):
    return pl.pallas_call(
        functools.partial(loadings_kernel, values),
        out_shape=jax.ShapeDtypeStruct(shape, F32),
        compiler_params=params(),
        name="next_loadings",
    )(v, grad, kept, got, traces, mine, other)


def invert(gram):
    rank = gram.shape[0]
    row = lax.broadcasted_iota(jnp.int32, (rank, rank), 0)
    col = lax.broadcasted_iota(jnp.int32, (rank, rank), 1)
    lane = lax.broadcasted_iota(jnp.int32, (1, rank), 1)
    diag = row == col
    trace = jnp.sum(jnp.where(diag, gram, 0.0))
    a = gram + jnp.where(diag, 0.1 * (trace / rank), 0.0)
    for k in range(0, rank, 2):
        row0, row1 = a[k : k + 1, :], a[k + 1 : k + 2, :]
        col0, col1 = a[:, k : k + 1], a[:, k + 1 : k + 2]
        p, q, r = a[k : k + 1, k : k + 1], a[k : k + 1, k + 1 : k + 2], a[k + 1 : k + 2, k + 1 : k + 2]
        scale = 1.0 / (p * r - q * q)
        p, q, r = r * scale, -q * scale, p * scale
        new0, new1 = p * row0 + q * row1, q * row0 + r * row1
        rest = a - (col0 * new0 + col1 * new1)
        rest = jnp.where(col == k, col0 * p + col1 * q, jnp.where(col == k + 1, col0 * q + col1 * r, rest))
        new0 = jnp.where(lane == k, -p, jnp.where(lane == k + 1, -q, new0))
        new1 = jnp.where(lane == k, -q, jnp.where(lane == k + 1, -r, new1))
        a = jnp.where(row == k, new0, jnp.where(row == k + 1, new1, rest))
    return -a


def inverse_kernel(cells, mine, other, hinv):
    hinv[...] = invert((mine[...] + other[...])[:, cells : cells + mine.shape[0]])


def inverse_of(cells, mine, other):
    rank = mine.shape[0]
    return pl.pallas_call(
        functools.partial(inverse_kernel, cells),
        out_shape=jax.ShapeDtypeStruct((rank, rank), F32),
        compiler_params=params(),
        cost_estimate=cost(16384, 128, 1024),
        name="inverse",
    )(mine, other)


def next_kernel(size_row, u, mine, other, hinv, vc, w1, w2, st1, st2, grad, u_out, weights, eb):
    rank, cells = u.shape
    total = mine[:, :cells] + other[:, :cells]
    now = u[...] - 0.25 * jnp.dot(hinv[...], total, precision=HIGH, preferred_element_type=F32)
    u_out[...] = now
    weights[...] = factor_operand(now, size_row[...])
    half = eb.shape[1]
    work = [(w, st, at) for w, st in ((w1, st1), (w2, st2)) for at in range(0, st.shape[1], 2 * half)]

    def front(i):
        w, _, at = work[i]
        eb[i % 2] = dot(w[at // 2 : at // 2 + half, :], weights[...])

    acc = jnp.zeros((2 * rank, 2 * cells), F32)
    front(0)
    for i, (_, st, at) in enumerate(work):
        if i + 1 < len(work):
            front(i + 1)
        acc = acc + dot(st[:, at : at + 2 * half], pairs(*split(jnp.exp2(eb[i % 2]), 2)))
    g = fold(acc, rank)
    grad[...] = g[:, :cells] + g[:, cells:] - vc[...]


def next_turn(width, size_row, u, mine, other, hinv, vc, w1, w2, st1, st2):
    rank, cells = u.shape
    return pl.pallas_call(
        next_kernel,
        out_shape=[jax.ShapeDtypeStruct((rank, cells), F32)] * 2,
        scratch_shapes=[
            pltpu.VMEM((256, 2 * cells), BF16),
            pltpu.VMEM((2, width, 2 * cells), F32),
        ],
        compiler_params=params(),
        cost_estimate=cost(2 * st1.shape[1], cells, 1024),
        name="next_turn",
    )(size_row, u, mine, other, hinv, vc, w1, w2, st1, st2)


def last_kernel(u, mine, other, hinv, u_out):
    total = mine[...] + other[...]
    u_out[...] = u[...] - 0.25 * jnp.dot(hinv[...], total, precision=HIGH, preferred_element_type=F32)


def last_update(u, mine, other, hinv):
    return pl.pallas_call(
        last_kernel,
        out_shape=jax.ShapeDtypeStruct(u.shape, F32),
        compiler_params=params(),
        name="last_update",
    )(u, mine, other, hinv)


def step_kernel(width, u, mine, other, hinv, size_row, v, cb0, cb1, u_out, message, uc0, uc1):
    rank = u.shape[0]
    total = mine[...] + other[...]
    now = u[...] - 0.25 * jnp.dot(hinv[...], total, precision=HIGH, preferred_element_type=F32)
    u_out[...] = now
    message[...] = message_of(now, size_row[...], v[...])
    left = jnp.concatenate(split(now, 2), 0)
    for cb, uc in ((cb1, uc1), (cb0, uc0)):
        for block in range(cb.shape[1] // width):
            c = cb[:, block * width : (block + 1) * width]
            uc[block * rank : (block + 1) * rank, :] = fold(dot(left, c), rank)


def step_update(width, u, mine, other, hinv, size_row, v, cb0, cb1):
    rank, cells = u.shape
    sums = jax.ShapeDtypeStruct((cb0.shape[1] // width * rank, width), F32)
    return pl.pallas_call(
        functools.partial(step_kernel, width),
        out_shape=[
            jax.ShapeDtypeStruct((rank, cells), F32),
            jax.ShapeDtypeStruct((rank + 8, cells), F32),
            sums,
            sums,
        ],
        compiler_params=params(),
        cost_estimate=cost(2 * cb0.shape[1], cells, 256),
        name="step_update",
    )(u, mine, other, hinv, size_row, v, cb0, cb1)


def params():
    return pltpu.CompilerParams(vmem_limit_bytes=VMEM_LIMIT)


def cost(genes, cells, depth):
    return pl.CostEstimate(flops=genes * cells * depth // 16, bytes_accessed=genes * cells // 4, transcendentals=genes * cells // 16)


def solution(mesh):
    n_cell = mesh.shape["cell"]
    n_gene = mesh.shape["gene"]
    bits = [1 << b for b in range(n_cell.bit_length() - 1)][::-1]
    far, near = bits[:-2], bits[-2:]
    orders = far + near, far[::-1] + near[::-1]
    rounds = len(bits)

    def swap(x, step):
        perm = [
            (i * n_gene + g, (i ^ orders[g % 2][step]) * n_gene + g) for i in range(n_cell) for g in range(n_gene)
        ]
        return lax.ppermute(x, ("cell", "gene"), perm)

    def sum_gene(x):
        for step in range(n_gene.bit_length() - 2, -1, -1):
            got = lax.ppermute(x, "gene", [(g, g ^ (1 << step)) for g in range(n_gene)])
            if step:
                x = x + got
        return x, got

    def masks(order):
        out = [0]
        for bit in order:
            out = out + [i | bit for i in out]
        return out

    def on_device(counts, size_factor, gene_offset, factors, loadings):
        rank, cells = factors.shape
        width = loadings.shape[2]
        slab = width * n_cell
        size_row = size_factor.reshape(1, -1)
        gene_row = gene_offset.reshape(1, -1)
        direct = width % 256 == 0
        block = width if direct else slab // 4
        if direct:
            half = n_cell // 2
            even, odd = [masks(o) for o in orders]
            owners = (even[:half], odd[:half]), (even[half:], odd[half:])
            own_row = gene_row
        else:
            owners = ([0, 1], None), ([2, 3], None)
            own_row = lax.dynamic_slice_in_dim(gene_row, lax.axis_index("cell") * width, width, 1)

        def double(x, step):
            return jnp.concatenate([x, swap(x, step)], 0)

        def halve(x, step):
            rows = x.shape[0] // 2
            return x[:rows], swap(x[rows:], step)

        def together(*xs):
            return lax.optimization_barrier(xs)

        def gather_plain(x):
            x = lax.all_gather(x, "cell", axis=1, tiled=True)
            x = x.reshape(rank, 2, 2, block).transpose(1, 2, 0, 3).reshape(2, 2 * rank, block)
            return x[0], x[1]

        def scatter_plain(x0, x1):
            x = jnp.stack([x0, x1]).reshape(4, rank, block).transpose(1, 0, 2).reshape(rank, slab)
            x = lax.psum_scatter(x, "cell", scatter_dimension=1, tiled=True)
            return x, jnp.zeros_like(x)

        def first_exchange(v, message):
            uc1, cb1 = first_counts(owners[1], counts, u, block, 57)
            got = swap(uc1, rounds - 1)
            b, g = v, message
            for step in range(len(far)):
                b, g = double(b, step), double(g, step)
            a, cb0 = first_counts(owners[0], counts, u, block, 50)
            for step in range(len(far), rounds - 1):
                g = double(g, step)
            a, got, b, g = together(a, got, b, g)
            last = swap(g, rounds - 1)
            for step in range(len(far), rounds - 1):
                a, got = halve(a + got, rounds - 2 - step + len(far))
                b = double(b, step)
                a, got, b, last = together(a, got, b, last)
            grad_v, traces = own_gradient(v, own_row, jnp.concatenate([g, last], 0))
            traces = traces, *sum_gene(traces)
            p1 = swap(b, rounds - 1)
            begun = start_part(owners[0], gene_row, size_row, u, b, cb0)
            for step in range(rounds - 1 - len(near), -1, -1):
                a, got = halve(a + got, step)
                if step:
                    a, got, grad_v, traces, begun = together(a, got, grad_v, traces, begun)
            return (cb0, cb1), p1, begun, grad_v, traces, a, got

        def plain_exchange(v, message, uc0, uc1):
            g = lax.all_gather(message, "cell", axis=0, tiled=True)
            return *own_gradient(v, own_row, g), *scatter_plain(uc0, uc1)

        u = factors
        v, message = entry(size_row, u, loadings)
        for step in range(ITERS):
            if not direct:
                if step == 0:
                    uc1, cb1 = first_counts(owners[1], counts, u, block)
                    uc0, cb0 = first_counts(owners[0], counts, u, block)
                p0, p1 = gather_plain(v)
                grad_v, traces, kept, got = plain_exchange(v, message, uc0, uc1)
                traces = traces, *sum_gene(traces)
                begun = start_part(owners[0], gene_row, size_row, u, p0, cb0)
            elif step == 0:
                (cb0, cb1), p1, begun, grad_v, traces, kept, got = first_exchange(v, message)
            else:
                begun = start_part(owners[0], gene_row, size_row, u, p0, cb0)
                p1, *begun = together(p1, *begun)
                uc1, p1 = together(uc1, p1)
                kept, got = uc0, swap(uc1, rounds - 1)

            def loadings_now(kept, got):
                shape = v.shape if step < ITERS - 1 else (rank, 1, width)
                return next_loadings(rank * slab * n_gene, shape, v, grad_v, kept, got, *traces)

            if not direct:
                v = loadings_now(kept, got)
                beside = lambda x, turn: x
            elif step < ITERS - 1:
                v = loadings_now(kept, got)
                state = {"held": v}

                def beside(x, turn):
                    if turn < rounds - 1:
                        x, got = together(x, swap(state["held"], turn))
                        state["held"] = jnp.concatenate([state["held"], got], 0)
                    if turn == rounds - 2:
                        state["last"] = swap(state["held"], rounds - 1)
                    return x
            else:
                state = {"kept": kept, "got": got, "step": rounds - 2, "message": message, "doubled": 0}

                def halve_on(x):
                    x, kept, got = together(x, state["kept"], state["got"])
                    state["kept"], state["got"] = halve(kept + got, state["step"])
                    state["step"] -= 1
                    return x

                def double_on(x):
                    x, got = together(x, swap(state["message"], state["doubled"]))
                    state["message"] = jnp.concatenate([state["message"], got], 0)
                    state["doubled"] += 1
                    return x

                def beside(x, turn):
                    if turn < rounds - 1:
                        x = double_on(x)
                    return halve_on(x) if turn == 2 else x

            w1, st1, *sums = begun
            w2, st2, packed, vc = start_part(owners[1], gene_row, size_row, u, p1, cb1, sums)
            mine, other = sum_gene(packed)
            mine = beside(mine, 0)
            hinv = beside(inverse_of(cells, mine, other), 1)
            for turn in range(2, FACTOR_STEPS + 1):
                mine, u = next_turn(block, size_row, u, mine, other, hinv, vc, w1, w2, st1, st2)
                mine, other = sum_gene(mine)
                if turn < FACTOR_STEPS:
                    mine = beside(mine, turn)
            if step < ITERS - 1:
                u, message, uc0, uc1 = step_update(block, u, mine, other, hinv, size_row, v, cb0, cb1)
            else:
                u = last_update(u, mine, other, hinv)
            if direct and step == ITERS - 1:
                mine = halve_on(mine)
                while state["doubled"] < rounds:
                    mine = double_on(mine)
                grad_v, traces = own_gradient(v, own_row, state["message"])
                traces = traces, *sum_gene(traces)
                while state["step"] >= 0:
                    grad_v = halve_on(grad_v)
            elif direct:
                for turn in range(FACTOR_STEPS, rounds - 1):
                    mine = beside(mine, turn)
            if direct and step < ITERS - 1:
                p0, p1 = state["held"], state["last"]
            elif direct:
                v = loadings_now(state["kept"], state["got"])
        return (u, v.reshape(rank, 1, width))

    return jax.shard_map(
        on_device,
        mesh=mesh,
        in_specs=(
            P("cell", "gene"),
            P("cell"),
            P("gene"),
            P(None, "cell"),
            P(None, "gene", "cell"),
        ),
        out_specs=(P(None, "cell"), P(None, "gene", "cell")),
        check_vma=False,
    )
```

```python
import functools
import math

import jax
import jax.numpy as jnp
from jax import lax
from jax.experimental import pallas as pl
from jax.experimental.pallas import tpu as pltpu
from jax.sharding import PartitionSpec as P

ITERS = 2
FACTOR_STEPS = 4
LOG2E = math.log2(math.e)
HIGH = lax.Precision.HIGHEST
F32 = jnp.float32
BF16 = jnp.bfloat16
VMEM_LIMIT = 14 * 1024 * 1024
NT = (((1,), (1,)), ((), ()))


def split(x, n):
    parts = []
    for i in range(n):
        part = x.astype(BF16)
        parts.append(part)
        if i < n - 1:
            x = x - part.astype(F32)
    return parts


def dot(a, b):
    return jnp.dot(a, b, preferred_element_type=F32)


def dot_nt(a, b):
    return lax.dot_general(a, b, NT, preferred_element_type=F32)


def factor_operand(u, size_row):
    rank, cells = u.shape
    u1, u2 = [p.astype(F32) for p in split(u * LOG2E, 2)]
    offsets = [p.astype(F32) for p in split(jnp.log(size_row.astype(F32) / 2000.0) * LOG2E, 3)]
    row = lax.broadcasted_iota(jnp.int32, (128 - 3 * rank, cells), 0)
    extra = jnp.where(row < 3, 1.0, 0.0)
    for i, o in enumerate(offsets):
        extra = jnp.where(row == 3 + i, o, extra)
    one = jnp.concatenate([u1, u1, u2, extra], 0)
    none = jnp.zeros_like(one)
    return jnp.concatenate([jnp.concatenate([one, none], 1), jnp.concatenate([none, one], 1)], 0).astype(BF16)


def gene_operand(v1, v2, gene_row):
    rank, genes = v1.shape
    row = lax.broadcasted_iota(jnp.int32, (128 - 3 * rank, genes), 0)
    extra = jnp.where(row < 6, 1.0, 0.0)
    for i, g in enumerate(split(gene_row * LOG2E, 3)):
        extra = jnp.where(row == i, g.astype(F32), extra)
    return jnp.concatenate([v1, v2, v1, extra.astype(BF16)], 0)


def fold(acc, rank):
    return acc[:rank] + acc[rank:]


def owner_of(owners, block):
    if owners[1] is None:
        return owners[0][block]
    even, odd = owners[0][block], owners[1][block]
    mask = jnp.where(lax.axis_index("gene") % 2 == 1, odd, even)
    return lax.axis_index("cell") ^ mask


def columns_of(owners, block, width):
    start = owner_of(owners, block) * width
    return pl.ds(start if isinstance(start, int) else pl.multiple_of(start, 128), width)


def counts_kernel(owners, counts, u, uc, cb, landed, sems):
    rank = u.shape[0]
    blocks, _, width = landed.shape
    copies = [
        pltpu.make_async_copy(counts.at[:, columns_of(owners, i, width)], landed.at[i], sems.at[i]) for i in range(blocks)
    ]
    for copy in copies:
        copy.start()
    left = jnp.concatenate(split(u[...], 2), 0)
    for i, copy in enumerate(copies):
        copy.wait()
        c = landed[i].astype(F32).astype(BF16)
        cb[:, i * width : (i + 1) * width] = c
        uc[i * rank : (i + 1) * rank, :] = fold(dot(left, c), rank)


def first_counts(owners, counts, u, width, room=14):
    rank, cells = u.shape
    blocks = len(owners[0])
    vmem = pl.BlockSpec(memory_space=pltpu.VMEM)
    return pl.pallas_call(
        functools.partial(counts_kernel, owners),
        in_specs=[pl.BlockSpec(memory_space=pltpu.HBM), vmem],
        out_specs=[vmem] * 2,
        out_shape=[
            jax.ShapeDtypeStruct((blocks * rank, width), F32),
            jax.ShapeDtypeStruct((cells, blocks * width), BF16),
        ],
        scratch_shapes=[pltpu.VMEM((blocks, cells, width), jnp.int32), pltpu.SemaphoreType.DMA((blocks,))],
        compiler_params=pltpu.CompilerParams(vmem_limit_bytes=room * 1024 * 1024),
        cost_estimate=cost(blocks * width, cells, 512),
        name="first_counts",
    )(counts, u)


def message_of(u, size_row, v):
    row = lax.broadcasted_iota(jnp.int32, (8, u.shape[1]), 0)
    return jnp.concatenate([u, jnp.where(row == 0, size_row.astype(F32), jnp.sum(v * v))], 0)


def entry_kernel(size_row, u, raw, v_out, message):
    v = raw[...].reshape(v_out.shape)
    v_out[...] = v
    message[...] = message_of(u[...], size_row[...], v)


def entry(size_row, u, raw):
    rank, cells = u.shape
    return pl.pallas_call(
        entry_kernel,
        out_shape=[
            jax.ShapeDtypeStruct((rank, raw.shape[2]), F32),
            jax.ShapeDtypeStruct((rank + 8, cells), F32),
        ],
        compiler_params=params(),
        name="entry",
    )(size_row, u, raw)


def pairs(e1, e2):
    cells = e1.shape[1] // 2
    top = jnp.concatenate([e1[:, :cells], e2[:, :cells]], 1)
    bottom = jnp.concatenate([e1[:, cells:], e2[:, cells:]], 1)
    return jnp.concatenate([top, bottom], 0)


def start_kernel(last, owners, gene_row, size_row, u_ref, v, cb, *refs):
    if last:
        gu_in, rest_in, w, st, packed, vc, weights, eb = refs
    else:
        w, st, gu_out, rest_out, weights, eb = refs
    u = u_ref[...]
    rank, cells = u.shape
    blocks, width = v.shape[0] // rank, v.shape[1]
    groups = blocks // 2
    weights[...] = factor_operand(u, size_row[...])
    gu = gu_in[...] if last else jnp.zeros((2 * rank, 2 * cells), F32)
    rest = rest_in[...] if last else jnp.zeros((2 * rank, cells + 2 * rank), F32)

    def prepare(i):
        for j in range(2):
            block = 2 * i + j
            v1, v2 = split(v[block * rank : (block + 1) * rank, :], 2)
            st[:, block * width : (block + 1) * width] = jnp.concatenate([v1, v2], 0)
            genes = gene_row[:, columns_of(owners, block, width)]
            w[i * width : (i + 1) * width, 128 * j : 128 * (j + 1)] = gene_operand(v1, v2, genes).T

    def front(i):
        eb[i % 2] = dot(w[i * width : (i + 1) * width, :], weights[...])

    for i in range(groups + 2):
        if i < groups:
            prepare(i)
        if 1 <= i <= groups:
            front(i - 1)
        if i >= 2:
            at = (i - 2) * 2 * width
            s = st[:, at : at + 2 * width]
            gu = gu + dot(s, pairs(*split(jnp.exp2(eb[i % 2]), 2)))
            rest = rest + dot_nt(s, jnp.concatenate([cb[:, at : at + 2 * width], s], 0))
    if not last:
        gu_out[...] = gu
        rest_out[...] = rest
        return
    gu, rest = fold(gu, rank), fold(rest, rank)
    vc[...] = rest[:, :cells]
    packed[:, :cells] = gu[:, :cells] + gu[:, cells:] - rest[:, :cells]
    gram = rest[:, cells : cells + rank] + rest[:, cells + rank :]
    packed[:, cells:] = jnp.concatenate([gram, jnp.zeros((rank, packed.shape[1] - cells - rank), F32)], 1)


def start_part(owners, gene_row, size_row, u, v, cb, sums=()):
    rank, cells = u.shape
    width = v.shape[1]
    genes = v.shape[0] // rank * width
    last = bool(sums)
    vmem = pl.BlockSpec(memory_space=pltpu.VMEM)
    shapes = ((rank, cells + 128), (rank, cells)) if last else ((2 * rank, 2 * cells), (2 * rank, cells + 2 * rank))
    return pl.pallas_call(
        functools.partial(start_kernel, last, owners),
        in_specs=[vmem] * (5 + len(sums)),
        out_specs=[vmem] * 4,
        out_shape=[
            jax.ShapeDtypeStruct((genes // 2, 256), BF16),
            jax.ShapeDtypeStruct((2 * rank, genes), BF16),
        ]
        + [jax.ShapeDtypeStruct(shape, F32) for shape in shapes],
        scratch_shapes=[
            pltpu.VMEM((256, 2 * cells), BF16),
            pltpu.VMEM((2, width, 2 * cells), F32),
        ],
        compiler_params=params(),
        cost_estimate=cost(genes, cells, 1024),
        name="start_part",
    )(gene_row, size_row, u, v, cb, *sums)


def own_kernel(v_ref, gene_row, u_all, grad, traces, eb):
    v = v_ref[...]
    rank, genes = v.shape
    rows = rank + 8
    blocks = u_all.shape[0] // rows
    v1, v2 = split(v, 2)
    place = lax.axis_index("cell") * genes
    own = slice(None) if gene_row.shape[1] == genes else pl.ds(pl.multiple_of(place, 128), genes)
    op = gene_operand(v1, v2, gene_row[:, own]).T
    w = jnp.concatenate([op[: genes // 2], op[genes // 2 :]], 1)
    g = jnp.zeros((2 * rank, genes), F32)
    trace_u = jnp.zeros((1, 1), F32)
    trace_v = jnp.zeros((1, 1), F32)

    def front(i):
        u = u_all[i * rows : i * rows + rank, :]
        eb[i % 2] = dot(w, factor_operand(u, u_all[i * rows + rank : i * rows + rank + 1, :]))

    front(0)
    for i in range(blocks):
        if i + 1 < blocks:
            front(i + 1)
        u = u_all[i * rows : i * rows + rank, :]
        left = jnp.concatenate(split(u, 2), 0)
        g = g + dot_nt(jnp.concatenate([left, left], 1), pairs(*split(jnp.exp2(eb[i % 2]), 2)))
        trace_u = trace_u + jnp.sum(u * u)
        trace_v = trace_v + u_all[i * rows + rank + 1 : i * rows + rank + 2, :1]
    grad[...] = fold(g, rank)
    row = lax.broadcasted_iota(jnp.int32, (8, 128), 0)
    traces[...] = jnp.where(row == 0, trace_u, trace_v)


def own_gradient(v, gene_row, u_all):
    rank, genes = v.shape
    return pl.pallas_call(
        own_kernel,
        out_shape=[jax.ShapeDtypeStruct(v.shape, F32), jax.ShapeDtypeStruct((8, 128), F32)],
        scratch_shapes=[pltpu.VMEM((2, genes // 2, 256), F32)],
        compiler_params=params(),
        cost_estimate=cost(genes, u_all.shape[0] // (rank + 8) * 128, 1024),
        name="own_gradient",
    )(v, gene_row, u_all)


def loadings_kernel(values, v, grad, kept, got, traces, mine, other, out):
    rank = v.shape[0]
    rate = 0.5 * rank / traces[0:1, 0:1]
    level = 0.1 * jnp.sqrt((mine[1:2, 0:1] + other[1:2, 0:1]) / values + 1e-06)
    moved = v[...] - rate * (grad[...] - (kept[...] + got[...]))
    less = jnp.maximum(jnp.abs(moved) - level, 0.0) / 1.1
    out[...] = jnp.where(moved < 0.0, -less, less).reshape(out.shape)


def next_loadings(values, shape, v, grad, kept, got, traces, mine, other):
    return pl.pallas_call(
        functools.partial(loadings_kernel, values),
        out_shape=jax.ShapeDtypeStruct(shape, F32),
        compiler_params=params(),
        name="next_loadings",
    )(v, grad, kept, got, traces, mine, other)


def invert(gram):
    rank = gram.shape[0]
    row = lax.broadcasted_iota(jnp.int32, (rank, rank), 0)
    col = lax.broadcasted_iota(jnp.int32, (rank, rank), 1)
    lane = lax.broadcasted_iota(jnp.int32, (1, rank), 1)
    diag = row == col
    trace = jnp.sum(jnp.where(diag, gram, 0.0))
    a = gram + jnp.where(diag, 0.1 * (trace / rank), 0.0)
    for k in range(0, rank, 2):
        row0, row1 = a[k : k + 1, :], a[k + 1 : k + 2, :]
        col0, col1 = a[:, k : k + 1], a[:, k + 1 : k + 2]
        p, q, r = a[k : k + 1, k : k + 1], a[k : k + 1, k + 1 : k + 2], a[k + 1 : k + 2, k + 1 : k + 2]
        scale = 1.0 / (p * r - q * q)
        p, q, r = r * scale, -q * scale, p * scale
        new0, new1 = p * row0 + q * row1, q * row0 + r * row1
        rest = a - (col0 * new0 + col1 * new1)
        rest = jnp.where(col == k, col0 * p + col1 * q, jnp.where(col == k + 1, col0 * q + col1 * r, rest))
        new0 = jnp.where(lane == k, -p, jnp.where(lane == k + 1, -q, new0))
        new1 = jnp.where(lane == k, -q, jnp.where(lane == k + 1, -r, new1))
        a = jnp.where(row == k, new0, jnp.where(row == k + 1, new1, rest))
    return -a


def inverse_kernel(cells, mine, other, hinv):
    hinv[...] = invert((mine[...] + other[...])[:, cells : cells + mine.shape[0]])


def inverse_of(cells, mine, other):
    rank = mine.shape[0]
    return pl.pallas_call(
        functools.partial(inverse_kernel, cells),
        out_shape=jax.ShapeDtypeStruct((rank, rank), F32),
        compiler_params=params(),
        cost_estimate=cost(16384, 128, 1024),
        name="inverse",
    )(mine, other)


def next_kernel(size_row, u, mine, other, hinv, vc, w1, w2, st1, st2, grad, u_out, weights, eb):
    rank, cells = u.shape
    total = mine[:, :cells] + other[:, :cells]
    now = u[...] - 0.25 * jnp.dot(hinv[...], total, precision=HIGH, preferred_element_type=F32)
    u_out[...] = now
    weights[...] = factor_operand(now, size_row[...])
    half = eb.shape[1]
    work = [(w, st, at) for w, st in ((w1, st1), (w2, st2)) for at in range(0, st.shape[1], 2 * half)]

    def front(i):
        w, _, at = work[i]
        eb[i % 2] = dot(w[at // 2 : at // 2 + half, :], weights[...])

    acc = jnp.zeros((2 * rank, 2 * cells), F32)
    front(0)
    for i, (_, st, at) in enumerate(work):
        if i + 1 < len(work):
            front(i + 1)
        acc = acc + dot(st[:, at : at + 2 * half], pairs(*split(jnp.exp2(eb[i % 2]), 2)))
    g = fold(acc, rank)
    grad[...] = g[:, :cells] + g[:, cells:] - vc[...]


def next_turn(width, size_row, u, mine, other, hinv, vc, w1, w2, st1, st2):
    rank, cells = u.shape
    return pl.pallas_call(
        next_kernel,
        out_shape=[jax.ShapeDtypeStruct((rank, cells), F32)] * 2,
        scratch_shapes=[
            pltpu.VMEM((256, 2 * cells), BF16),
            pltpu.VMEM((2, width, 2 * cells), F32),
        ],
        compiler_params=params(),
        cost_estimate=cost(2 * st1.shape[1], cells, 1024),
        name="next_turn",
    )(size_row, u, mine, other, hinv, vc, w1, w2, st1, st2)


def last_kernel(u, mine, other, hinv, u_out):
    total = mine[...] + other[...]
    u_out[...] = u[...] - 0.25 * jnp.dot(hinv[...], total, precision=HIGH, preferred_element_type=F32)


def last_update(u, mine, other, hinv):
    return pl.pallas_call(
        last_kernel,
        out_shape=jax.ShapeDtypeStruct(u.shape, F32),
        compiler_params=params(),
        name="last_update",
    )(u, mine, other, hinv)


def step_kernel(width, u, mine, other, hinv, size_row, v, cb0, cb1, u_out, message, uc0, uc1):
    rank = u.shape[0]
    total = mine[...] + other[...]
    now = u[...] - 0.25 * jnp.dot(hinv[...], total, precision=HIGH, preferred_element_type=F32)
    u_out[...] = now
    message[...] = message_of(now, size_row[...], v[...])
    left = jnp.concatenate(split(now, 2), 0)
    for cb, uc in ((cb1, uc1), (cb0, uc0)):
        for block in range(cb.shape[1] // width):
            c = cb[:, block * width : (block + 1) * width]
            uc[block * rank : (block + 1) * rank, :] = fold(dot(left, c), rank)


def step_update(width, u, mine, other, hinv, size_row, v, cb0, cb1):
    rank, cells = u.shape
    sums = jax.ShapeDtypeStruct((cb0.shape[1] // width * rank, width), F32)
    return pl.pallas_call(
        functools.partial(step_kernel, width),
        out_shape=[
            jax.ShapeDtypeStruct((rank, cells), F32),
            jax.ShapeDtypeStruct((rank + 8, cells), F32),
            sums,
            sums,
        ],
        compiler_params=params(),
        cost_estimate=cost(2 * cb0.shape[1], cells, 256),
        name="step_update",
    )(u, mine, other, hinv, size_row, v, cb0, cb1)


def params():
    return pltpu.CompilerParams(vmem_limit_bytes=VMEM_LIMIT)


def cost(genes, cells, depth):
    return pl.CostEstimate(flops=genes * cells * depth // 16, bytes_accessed=genes * cells // 4, transcendentals=genes * cells // 16)


def solution(mesh):
    n_cell = mesh.shape["cell"]
    n_gene = mesh.shape["gene"]
    bits = [1 << b for b in range(n_cell.bit_length() - 1)][::-1]
    far, near = bits[:-2], bits[-2:]
    orders = far + near, far[::-1] + near[::-1]
    rounds = len(bits)

    def swap(x, step):
        perm = [
            (i * n_gene + g, (i ^ orders[g % 2][step]) * n_gene + g) for i in range(n_cell) for g in range(n_gene)
        ]
        return lax.ppermute(x, ("cell", "gene"), perm)

    def sum_gene(x):
        for step in range(n_gene.bit_length() - 2, -1, -1):
            got = lax.ppermute(x, "gene", [(g, g ^ (1 << step)) for g in range(n_gene)])
            if step:
                x = x + got
        return x, got

    def masks(order):
        out = [0]
        for bit in order:
            out = out + [i | bit for i in out]
        return out

    def on_device(counts, size_factor, gene_offset, factors, loadings):
        rank, cells = factors.shape
        width = loadings.shape[2]
        slab = width * n_cell
        size_row = size_factor.reshape(1, -1)
        gene_row = gene_offset.reshape(1, -1)
        direct = width % 256 == 0
        block = width if direct else slab // 4
        if direct:
            half = n_cell // 2
            even, odd = [masks(o) for o in orders]
            owners = (even[:half], odd[:half]), (even[half:], odd[half:])
            own_row = gene_row
        else:
            owners = ([0, 1], None), ([2, 3], None)
            own_row = lax.dynamic_slice_in_dim(gene_row, lax.axis_index("cell") * width, width, 1)

        def double(x, step):
            return jnp.concatenate([x, swap(x, step)], 0)

        def halve(x, step):
            rows = x.shape[0] // 2
            return x[:rows], swap(x[rows:], step)

        def together(*xs):
            return lax.optimization_barrier(xs)

        def gather_plain(x):
            x = lax.all_gather(x, "cell", axis=1, tiled=True)
            x = x.reshape(rank, 2, 2, block).transpose(1, 2, 0, 3).reshape(2, 2 * rank, block)
            return x[0], x[1]

        def scatter_plain(x0, x1):
            x = jnp.stack([x0, x1]).reshape(4, rank, block).transpose(1, 0, 2).reshape(rank, slab)
            x = lax.psum_scatter(x, "cell", scatter_dimension=1, tiled=True)
            return x, jnp.zeros_like(x)

        def first_exchange(v, message):
            uc1, cb1 = first_counts(owners[1], counts, u, block, 57)
            got = swap(uc1, rounds - 1)
            b, g = v, message
            for step in range(len(far)):
                b, g = double(b, step), double(g, step)
            a, cb0 = first_counts(owners[0], counts, u, block, 50)
            for step in range(len(far), rounds - 1):
                g = double(g, step)
            a, got, b, g = together(a, got, b, g)
            last = swap(g, rounds - 1)
            for step in range(len(far), rounds - 1):
                a, got = halve(a + got, rounds - 2 - step + len(far))
                b = double(b, step)
                a, got, b, last = together(a, got, b, last)
            grad_v, traces = own_gradient(v, own_row, jnp.concatenate([g, last], 0))
            traces = traces, *sum_gene(traces)
            p1 = swap(b, rounds - 1)
            begun = start_part(owners[0], gene_row, size_row, u, b, cb0)
            for step in range(rounds - 1 - len(near), -1, -1):
                a, got = halve(a + got, step)
                if step:
                    a, got, grad_v, traces, begun = together(a, got, grad_v, traces, begun)
            return (cb0, cb1), p1, begun, grad_v, traces, a, got

        def plain_exchange(v, message, uc0, uc1):
            g = lax.all_gather(message, "cell", axis=0, tiled=True)
            return *own_gradient(v, own_row, g), *scatter_plain(uc0, uc1)

        u = factors
        v, message = entry(size_row, u, loadings)
        for step in range(ITERS):
            if not direct:
                if step == 0:
                    uc1, cb1 = first_counts(owners[1], counts, u, block)
                    uc0, cb0 = first_counts(owners[0], counts, u, block)
                p0, p1 = gather_plain(v)
                grad_v, traces, kept, got = plain_exchange(v, message, uc0, uc1)
                traces = traces, *sum_gene(traces)
                begun = start_part(owners[0], gene_row, size_row, u, p0, cb0)
            elif step == 0:
                (cb0, cb1), p1, begun, grad_v, traces, kept, got = first_exchange(v, message)
            else:
                begun = start_part(owners[0], gene_row, size_row, u, p0, cb0)
                p1, *begun = together(p1, *begun)
                uc1, p1 = together(uc1, p1)
                kept, got = uc0, swap(uc1, rounds - 1)

            def loadings_now(kept, got):
                shape = v.shape if step < ITERS - 1 else (rank, 1, width)
                return next_loadings(rank * slab * n_gene, shape, v, grad_v, kept, got, *traces)

            if not direct:
                v = loadings_now(kept, got)
                beside = lambda x, turn: x
            elif step < ITERS - 1:
                v = loadings_now(kept, got)
                state = {"held": v}

                def beside(x, turn):
                    if turn < rounds - 1:
                        x, got = together(x, swap(state["held"], turn))
                        state["held"] = jnp.concatenate([state["held"], got], 0)
                    if turn == rounds - 2:
                        state["last"] = swap(state["held"], rounds - 1)
                    return x
            else:
                state = {"kept": kept, "got": got, "step": rounds - 2, "message": message, "doubled": 0}

                def halve_on(x):
                    x, kept, got = together(x, state["kept"], state["got"])
                    state["kept"], state["got"] = halve(kept + got, state["step"])
                    state["step"] -= 1
                    return x

                def double_on(x):
                    x, got = together(x, swap(state["message"], state["doubled"]))
                    state["message"] = jnp.concatenate([state["message"], got], 0)
                    state["doubled"] += 1
                    return x

                def beside(x, turn):
                    if turn != 2 and state["doubled"] < rounds - 1:
                        x = double_on(x)
                    return halve_on(x) if turn % 2 and state["step"] > 0 else x

            w1, st1, *sums = begun
            w2, st2, packed, vc = start_part(owners[1], gene_row, size_row, u, p1, cb1, sums)
            mine, other = sum_gene(packed)
            mine = beside(mine, 0)
            hinv = beside(inverse_of(cells, mine, other), 1)
            for turn in range(2, FACTOR_STEPS + 1):
                mine, u = next_turn(block, size_row, u, mine, other, hinv, vc, w1, w2, st1, st2)
                mine, other = sum_gene(mine)
                if turn < FACTOR_STEPS:
                    mine = beside(mine, turn)
            if step < ITERS - 1:
                u, message, uc0, uc1 = step_update(block, u, mine, other, hinv, size_row, v, cb0, cb1)
            else:
                u = last_update(u, mine, other, hinv)
            if direct and step == ITERS - 1:
                if state["step"] >= 0:
                    mine = halve_on(mine)
                while state["doubled"] < rounds:
                    mine = double_on(mine)
                grad_v, traces = own_gradient(v, own_row, state["message"])
                traces = traces, *sum_gene(traces)
                while state["step"] >= 0:
                    grad_v = halve_on(grad_v)
            elif direct:
                for turn in range(FACTOR_STEPS, rounds - 1):
                    mine = beside(mine, turn)
            if direct and step < ITERS - 1:
                p0, p1 = state["held"], state["last"]
            elif direct:
                v = loadings_now(state["kept"], state["got"])
        return (u, v.reshape(rank, 1, width))

    return jax.shard_map(
        on_device,
        mesh=mesh,
        in_specs=(
            P("cell", "gene"),
            P("cell"),
            P("gene"),
            P(None, "cell"),
            P(None, "gene", "cell"),
        ),
        out_specs=(P(None, "cell"), P(None, "gene", "cell")),
        check_vma=False,
    )
```

```python
import functools
import math

import jax
import jax.numpy as jnp
from jax import lax
from jax.experimental import pallas as pl
from jax.experimental.pallas import tpu as pltpu
from jax.sharding import PartitionSpec as P

ITERS = 2
FACTOR_STEPS = 4
LOG2E = math.log2(math.e)
HIGH = lax.Precision.HIGHEST
F32 = jnp.float32
BF16 = jnp.bfloat16
VMEM_LIMIT = 14 * 1024 * 1024
NT = (((1,), (1,)), ((), ()))


def split(x, n):
    parts = []
    for i in range(n):
        part = x.astype(BF16)
        parts.append(part)
        if i < n - 1:
            x = x - part.astype(F32)
    return parts


def dot(a, b):
    return jnp.dot(a, b, preferred_element_type=F32)


def dot_nt(a, b):
    return lax.dot_general(a, b, NT, preferred_element_type=F32)


def factor_operand(u, size_row):
    rank, cells = u.shape
    u1, u2 = [p.astype(F32) for p in split(u * LOG2E, 2)]
    offsets = [p.astype(F32) for p in split(jnp.log(size_row.astype(F32) / 2000.0) * LOG2E, 3)]
    row = lax.broadcasted_iota(jnp.int32, (128 - 3 * rank, cells), 0)
    extra = jnp.where(row < 3, 1.0, 0.0)
    for i, o in enumerate(offsets):
        extra = jnp.where(row == 3 + i, o, extra)
    one = jnp.concatenate([u1, u1, u2, extra], 0)
    none = jnp.zeros_like(one)
    return jnp.concatenate([jnp.concatenate([one, none], 1), jnp.concatenate([none, one], 1)], 0).astype(BF16)


def gene_operand(v1, v2, gene_row):
    rank, genes = v1.shape
    row = lax.broadcasted_iota(jnp.int32, (128 - 3 * rank, genes), 0)
    extra = jnp.where(row < 6, 1.0, 0.0)
    for i, g in enumerate(split(gene_row * LOG2E, 3)):
        extra = jnp.where(row == i, g.astype(F32), extra)
    return jnp.concatenate([v1, v2, v1, extra.astype(BF16)], 0)


def fold(acc, rank):
    return acc[:rank] + acc[rank:]


def owner_of(owners, block):
    if owners[1] is None:
        return owners[0][block]
    even, odd = owners[0][block], owners[1][block]
    mask = jnp.where(lax.axis_index("gene") % 2 == 1, odd, even)
    return lax.axis_index("cell") ^ mask


def columns_of(owners, block, width):
    start = owner_of(owners, block) * width
    return pl.ds(start if isinstance(start, int) else pl.multiple_of(start, 128), width)


def counts_kernel(owners, counts, u, uc, cb, landed, sems):
    rank = u.shape[0]
    blocks, _, width = landed.shape
    copies = [
        pltpu.make_async_copy(counts.at[:, columns_of(owners, i, width)], landed.at[i], sems.at[i]) for i in range(blocks)
    ]
    for copy in copies:
        copy.start()
    left = jnp.concatenate(split(u[...], 2), 0)
    for i, copy in enumerate(copies):
        copy.wait()
        c = landed[i].astype(F32).astype(BF16)
        cb[:, i * width : (i + 1) * width] = c
        uc[i * rank : (i + 1) * rank, :] = fold(dot(left, c), rank)


def first_counts(owners, counts, u, width, room=14):
    rank, cells = u.shape
    blocks = len(owners[0])
    vmem = pl.BlockSpec(memory_space=pltpu.VMEM)
    return pl.pallas_call(
        functools.partial(counts_kernel, owners),
        in_specs=[pl.BlockSpec(memory_space=pltpu.HBM), vmem],
        out_specs=[vmem] * 2,
        out_shape=[
            jax.ShapeDtypeStruct((blocks * rank, width), F32),
            jax.ShapeDtypeStruct((cells, blocks * width), BF16),
        ],
        scratch_shapes=[pltpu.VMEM((blocks, cells, width), jnp.int32), pltpu.SemaphoreType.DMA((blocks,))],
        compiler_params=pltpu.CompilerParams(vmem_limit_bytes=room * 1024 * 1024),
        cost_estimate=cost(blocks * width, cells, 512),
        name="first_counts",
    )(counts, u)


def message_of(u, size_row, v):
    row = lax.broadcasted_iota(jnp.int32, (8, u.shape[1]), 0)
    return jnp.concatenate([u, jnp.where(row == 0, size_row.astype(F32), jnp.sum(v * v))], 0)


def entry_kernel(size_row, u, raw, v_out, message):
    v = raw[...].reshape(v_out.shape)
    v_out[...] = v
    message[...] = message_of(u[...], size_row[...], v)


def entry(size_row, u, raw):
    rank, cells = u.shape
    return pl.pallas_call(
        entry_kernel,
        out_shape=[
            jax.ShapeDtypeStruct((rank, raw.shape[2]), F32),
            jax.ShapeDtypeStruct((rank + 8, cells), F32),
        ],
        compiler_params=params(),
        name="entry",
    )(size_row, u, raw)


def pairs(e1, e2):
    cells = e1.shape[1] // 2
    top = jnp.concatenate([e1[:, :cells], e2[:, :cells]], 1)
    bottom = jnp.concatenate([e1[:, cells:], e2[:, cells:]], 1)
    return jnp.concatenate([top, bottom], 0)


def start_kernel(last, owners, gene_row, size_row, u_ref, v, cb, *refs):
    if last:
        gu_in, rest_in, w, st, packed, vc, weights, eb = refs
    else:
        w, st, gu_out, rest_out, weights, eb = refs
    u = u_ref[...]
    rank, cells = u.shape
    blocks, width = v.shape[0] // rank, v.shape[1]
    groups = blocks // 2
    weights[...] = factor_operand(u, size_row[...])
    gu = gu_in[...] if last else jnp.zeros((2 * rank, 2 * cells), F32)
    rest = rest_in[...] if last else jnp.zeros((2 * rank, cells + 2 * rank), F32)

    def prepare(i):
        for j in range(2):
            block = 2 * i + j
            v1, v2 = split(v[block * rank : (block + 1) * rank, :], 2)
            st[:, block * width : (block + 1) * width] = jnp.concatenate([v1, v2], 0)
            genes = gene_row[:, columns_of(owners, block, width)]
            w[i * width : (i + 1) * width, 128 * j : 128 * (j + 1)] = gene_operand(v1, v2, genes).T

    def front(i):
        eb[i % 2] = dot(w[i * width : (i + 1) * width, :], weights[...])

    for i in range(groups + 2):
        if i < groups:
            prepare(i)
        if 1 <= i <= groups:
            front(i - 1)
        if i >= 2:
            at = (i - 2) * 2 * width
            s = st[:, at : at + 2 * width]
            gu = gu + dot(s, pairs(*split(jnp.exp2(eb[i % 2]), 2)))
            rest = rest + dot_nt(s, jnp.concatenate([cb[:, at : at + 2 * width], s], 0))
    if not last:
        gu_out[...] = gu
        rest_out[...] = rest
        return
    gu, rest = fold(gu, rank), fold(rest, rank)
    vc[...] = rest[:, :cells]
    packed[:, :cells] = gu[:, :cells] + gu[:, cells:] - rest[:, :cells]
    gram = rest[:, cells : cells + rank] + rest[:, cells + rank :]
    packed[:, cells:] = jnp.concatenate([gram, jnp.zeros((rank, packed.shape[1] - cells - rank), F32)], 1)


def start_part(owners, gene_row, size_row, u, v, cb, sums=()):
    rank, cells = u.shape
    width = v.shape[1]
    genes = v.shape[0] // rank * width
    last = bool(sums)
    vmem = pl.BlockSpec(memory_space=pltpu.VMEM)
    shapes = ((rank, cells + 128), (rank, cells)) if last else ((2 * rank, 2 * cells), (2 * rank, cells + 2 * rank))
    return pl.pallas_call(
        functools.partial(start_kernel, last, owners),
        in_specs=[vmem] * (5 + len(sums)),
        out_specs=[vmem] * 4,
        out_shape=[
            jax.ShapeDtypeStruct((genes // 2, 256), BF16),
            jax.ShapeDtypeStruct((2 * rank, genes), BF16),
        ]
        + [jax.ShapeDtypeStruct(shape, F32) for shape in shapes],
        scratch_shapes=[
            pltpu.VMEM((256, 2 * cells), BF16),
            pltpu.VMEM((2, width, 2 * cells), F32),
        ],
        compiler_params=params(),
        cost_estimate=cost(genes, cells, 1024),
        name="start_part",
    )(gene_row, size_row, u, v, cb, *sums)


def own_kernel(v_ref, gene_row, u_all, grad, traces, eb):
    v = v_ref[...]
    rank, genes = v.shape
    rows = rank + 8
    blocks = u_all.shape[0] // rows
    v1, v2 = split(v, 2)
    place = lax.axis_index("cell") * genes
    own = slice(None) if gene_row.shape[1] == genes else pl.ds(pl.multiple_of(place, 128), genes)
    op = gene_operand(v1, v2, gene_row[:, own]).T
    w = jnp.concatenate([op[: genes // 2], op[genes // 2 :]], 1)
    g = jnp.zeros((2 * rank, genes), F32)
    trace_u = jnp.zeros((1, 1), F32)
    trace_v = jnp.zeros((1, 1), F32)

    def front(i):
        u = u_all[i * rows : i * rows + rank, :]
        eb[i % 2] = dot(w, factor_operand(u, u_all[i * rows + rank : i * rows + rank + 1, :]))

    front(0)
    for i in range(blocks):
        if i + 1 < blocks:
            front(i + 1)
        u = u_all[i * rows : i * rows + rank, :]
        left = jnp.concatenate(split(u, 2), 0)
        g = g + dot_nt(jnp.concatenate([left, left], 1), pairs(*split(jnp.exp2(eb[i % 2]), 2)))
        trace_u = trace_u + jnp.sum(u * u)
        trace_v = trace_v + u_all[i * rows + rank + 1 : i * rows + rank + 2, :1]
    grad[...] = fold(g, rank)
    row = lax.broadcasted_iota(jnp.int32, (8, 128), 0)
    traces[...] = jnp.where(row == 0, trace_u, trace_v)


def own_gradient(v, gene_row, u_all):
    rank, genes = v.shape
    return pl.pallas_call(
        own_kernel,
        out_shape=[jax.ShapeDtypeStruct(v.shape, F32), jax.ShapeDtypeStruct((8, 128), F32)],
        scratch_shapes=[pltpu.VMEM((2, genes // 2, 256), F32)],
        compiler_params=params(),
        cost_estimate=cost(genes, u_all.shape[0] // (rank + 8) * 128, 1024),
        name="own_gradient",
    )(v, gene_row, u_all)


def loadings_kernel(values, v, grad, kept, got, traces, mine, other, out):
    rank = v.shape[0]
    rate = 0.5 * rank / traces[0:1, 0:1]
    level = 0.1 * jnp.sqrt((mine[1:2, 0:1] + other[1:2, 0:1]) / values + 1e-06)
    moved = v[...] - rate * (grad[...] - (kept[...] + got[...]))
    less = jnp.maximum(jnp.abs(moved) - level, 0.0) / 1.1
    out[...] = jnp.where(moved < 0.0, -less, less).reshape(out.shape)


def next_loadings(values, shape, v, grad, kept, got, traces, mine, other):
    return pl.pallas_call(
        functools.partial(loadings_kernel, values),
        out_shape=jax.ShapeDtypeStruct(shape, F32),
        compiler_params=params(),
        name="next_loadings",
    )(v, grad, kept, got, traces, mine, other)


def invert(gram):
    rank = gram.shape[0]
    row = lax.broadcasted_iota(jnp.int32, (rank, rank), 0)
    col = lax.broadcasted_iota(jnp.int32, (rank, rank), 1)
    lane = lax.broadcasted_iota(jnp.int32, (1, rank), 1)
    diag = row == col
    scale = rank / jnp.sum(jnp.where(diag, gram, 0.0))
    a = gram * scale + jnp.where(diag, 0.1, 0.0)
    for k in range(0, rank, 2):
        row0, row1 = a[k : k + 1, :], a[k + 1 : k + 2, :]
        col0, col1 = a[:, k : k + 1], a[:, k + 1 : k + 2]
        p, q, r = a[k : k + 1, k : k + 1], a[k : k + 1, k + 1 : k + 2], a[k + 1 : k + 2, k + 1 : k + 2]
        over = 1.0 / (p * r - q * q)
        p, q, r = r * over, -q * over, p * over
        new0, new1 = p * row0 + q * row1, q * row0 + r * row1
        rest = a - (col0 * new0 + col1 * new1)
        rest = jnp.where(col == k, col0 * p + col1 * q, jnp.where(col == k + 1, col0 * q + col1 * r, rest))
        new0 = jnp.where(lane == k, -p, jnp.where(lane == k + 1, -q, new0))
        new1 = jnp.where(lane == k, -q, jnp.where(lane == k + 1, -r, new1))
        a = jnp.where(row == k, new0, jnp.where(row == k + 1, new1, rest))
    return -a * scale


def inverse_kernel(cells, mine, other, hinv):
    hinv[...] = invert((mine[...] + other[...])[:, cells : cells + mine.shape[0]])


def inverse_of(cells, mine, other):
    rank = mine.shape[0]
    return pl.pallas_call(
        functools.partial(inverse_kernel, cells),
        out_shape=jax.ShapeDtypeStruct((rank, rank), F32),
        compiler_params=params(),
        cost_estimate=cost(16384, 128, 1024),
        name="inverse",
    )(mine, other)


def next_kernel(size_row, u, mine, other, hinv, vc, w1, w2, st1, st2, grad, u_out, weights, eb):
    rank, cells = u.shape
    total = mine[:, :cells] + other[:, :cells]
    now = u[...] - 0.25 * jnp.dot(hinv[...], total, precision=HIGH, preferred_element_type=F32)
    u_out[...] = now
    weights[...] = factor_operand(now, size_row[...])
    half = eb.shape[1]
    work = [(w, st, at) for w, st in ((w1, st1), (w2, st2)) for at in range(0, st.shape[1], 2 * half)]

    def front(i):
        w, _, at = work[i]
        eb[i % 2] = dot(w[at // 2 : at // 2 + half, :], weights[...])

    acc = jnp.zeros((2 * rank, 2 * cells), F32)
    front(0)
    for i, (_, st, at) in enumerate(work):
        if i + 1 < len(work):
            front(i + 1)
        acc = acc + dot(st[:, at : at + 2 * half], pairs(*split(jnp.exp2(eb[i % 2]), 2)))
    g = fold(acc, rank)
    grad[...] = g[:, :cells] + g[:, cells:] - vc[...]


def next_turn(width, size_row, u, mine, other, hinv, vc, w1, w2, st1, st2):
    rank, cells = u.shape
    return pl.pallas_call(
        next_kernel,
        out_shape=[jax.ShapeDtypeStruct((rank, cells), F32)] * 2,
        scratch_shapes=[
            pltpu.VMEM((256, 2 * cells), BF16),
            pltpu.VMEM((2, width, 2 * cells), F32),
        ],
        compiler_params=params(),
        cost_estimate=cost(2 * st1.shape[1], cells, 1024),
        name="next_turn",
    )(size_row, u, mine, other, hinv, vc, w1, w2, st1, st2)


def last_kernel(u, mine, other, hinv, u_out):
    total = mine[...] + other[...]
    u_out[...] = u[...] - 0.25 * jnp.dot(hinv[...], total, precision=HIGH, preferred_element_type=F32)


def last_update(u, mine, other, hinv):
    return pl.pallas_call(
        last_kernel,
        out_shape=jax.ShapeDtypeStruct(u.shape, F32),
        compiler_params=params(),
        name="last_update",
    )(u, mine, other, hinv)


def step_kernel(width, u, mine, other, hinv, size_row, v, cb0, cb1, u_out, message, uc0, uc1):
    rank = u.shape[0]
    total = mine[...] + other[...]
    now = u[...] - 0.25 * jnp.dot(hinv[...], total, precision=HIGH, preferred_element_type=F32)
    u_out[...] = now
    message[...] = message_of(now, size_row[...], v[...])
    left = jnp.concatenate(split(now, 2), 0)
    for cb, uc in ((cb1, uc1), (cb0, uc0)):
        for block in range(cb.shape[1] // width):
            c = cb[:, block * width : (block + 1) * width]
            uc[block * rank : (block + 1) * rank, :] = fold(dot(left, c), rank)


def step_update(width, u, mine, other, hinv, size_row, v, cb0, cb1):
    rank, cells = u.shape
    sums = jax.ShapeDtypeStruct((cb0.shape[1] // width * rank, width), F32)
    return pl.pallas_call(
        functools.partial(step_kernel, width),
        out_shape=[
            jax.ShapeDtypeStruct((rank, cells), F32),
            jax.ShapeDtypeStruct((rank + 8, cells), F32),
            sums,
            sums,
        ],
        compiler_params=params(),
        cost_estimate=cost(2 * cb0.shape[1], cells, 256),
        name="step_update",
    )(u, mine, other, hinv, size_row, v, cb0, cb1)


def params():
    return pltpu.CompilerParams(vmem_limit_bytes=VMEM_LIMIT)


def cost(genes, cells, depth):
    return pl.CostEstimate(flops=genes * cells * depth // 16, bytes_accessed=genes * cells // 4, transcendentals=genes * cells // 16)


def solution(mesh):
    n_cell = mesh.shape["cell"]
    n_gene = mesh.shape["gene"]
    bits = [1 << b for b in range(n_cell.bit_length() - 1)][::-1]
    far, near = bits[:-2], bits[-2:]
    orders = far + near, far[::-1] + near[::-1]
    rounds = len(bits)

    def swap(x, step):
        perm = [
            (i * n_gene + g, (i ^ orders[g % 2][step]) * n_gene + g) for i in range(n_cell) for g in range(n_gene)
        ]
        return lax.ppermute(x, ("cell", "gene"), perm)

    def sum_gene(x):
        for step in range(n_gene.bit_length() - 2, -1, -1):
            got = lax.ppermute(x, "gene", [(g, g ^ (1 << step)) for g in range(n_gene)])
            if step:
                x = x + got
        return x, got

    def masks(order):
        out = [0]
        for bit in order:
            out = out + [i | bit for i in out]
        return out

    def on_device(counts, size_factor, gene_offset, factors, loadings):
        rank, cells = factors.shape
        width = loadings.shape[2]
        slab = width * n_cell
        size_row = size_factor.reshape(1, -1)
        gene_row = gene_offset.reshape(1, -1)
        direct = width % 256 == 0
        block = width if direct else slab // 4
        if direct:
            half = n_cell // 2
            even, odd = [masks(o) for o in orders]
            owners = (even[:half], odd[:half]), (even[half:], odd[half:])
            own_row = gene_row
        else:
            owners = ([0, 1], None), ([2, 3], None)
            own_row = lax.dynamic_slice_in_dim(gene_row, lax.axis_index("cell") * width, width, 1)

        def double(x, step):
            return jnp.concatenate([x, swap(x, step)], 0)

        def halve(x, step):
            rows = x.shape[0] // 2
            return x[:rows], swap(x[rows:], step)

        def together(*xs):
            return lax.optimization_barrier(xs)

        def gather_plain(x):
            x = lax.all_gather(x, "cell", axis=1, tiled=True)
            x = x.reshape(rank, 2, 2, block).transpose(1, 2, 0, 3).reshape(2, 2 * rank, block)
            return x[0], x[1]

        def scatter_plain(x0, x1):
            x = jnp.stack([x0, x1]).reshape(4, rank, block).transpose(1, 0, 2).reshape(rank, slab)
            x = lax.psum_scatter(x, "cell", scatter_dimension=1, tiled=True)
            return x, jnp.zeros_like(x)

        def first_exchange(v, message):
            uc1, cb1 = first_counts(owners[1], counts, u, block, 57)
            got = swap(uc1, rounds - 1)
            b, g = v, message
            for step in range(len(far)):
                b, g = double(b, step), double(g, step)
            a, cb0 = first_counts(owners[0], counts, u, block, 50)
            for step in range(len(far), rounds - 1):
                g = double(g, step)
            a, got, b, g = together(a, got, b, g)
            last = swap(g, rounds - 1)
            for step in range(len(far), rounds - 1):
                a, got = halve(a + got, rounds - 2 - step + len(far))
                b = double(b, step)
                a, got, b, last = together(a, got, b, last)
            grad_v, traces = own_gradient(v, own_row, jnp.concatenate([g, last], 0))
            traces = traces, *sum_gene(traces)
            p1 = swap(b, rounds - 1)
            begun = start_part(owners[0], gene_row, size_row, u, b, cb0)
            for step in range(rounds - 1 - len(near), -1, -1):
                a, got = halve(a + got, step)
                if step:
                    a, got, grad_v, traces, begun = together(a, got, grad_v, traces, begun)
            return (cb0, cb1), p1, begun, grad_v, traces, a, got

        def plain_exchange(v, message, uc0, uc1):
            g = lax.all_gather(message, "cell", axis=0, tiled=True)
            return *own_gradient(v, own_row, g), *scatter_plain(uc0, uc1)

        u = factors
        v, message = entry(size_row, u, loadings)
        for step in range(ITERS):
            if not direct:
                if step == 0:
                    uc1, cb1 = first_counts(owners[1], counts, u, block)
                    uc0, cb0 = first_counts(owners[0], counts, u, block)
                p0, p1 = gather_plain(v)
                grad_v, traces, kept, got = plain_exchange(v, message, uc0, uc1)
                traces = traces, *sum_gene(traces)
                begun = start_part(owners[0], gene_row, size_row, u, p0, cb0)
            elif step == 0:
                (cb0, cb1), p1, begun, grad_v, traces, kept, got = first_exchange(v, message)
            else:
                begun = start_part(owners[0], gene_row, size_row, u, p0, cb0)
                p1, *begun = together(p1, *begun)
                uc1, p1 = together(uc1, p1)
                kept, got = uc0, swap(uc1, rounds - 1)

            def loadings_now(kept, got):
                shape = v.shape if step < ITERS - 1 else (rank, 1, width)
                return next_loadings(rank * slab * n_gene, shape, v, grad_v, kept, got, *traces)

            if not direct:
                v = loadings_now(kept, got)
                beside = lambda x, turn: x
            elif step < ITERS - 1:
                v = loadings_now(kept, got)
                state = {"held": v}

                def beside(x, turn):
                    if turn < rounds - 1:
                        x, got = together(x, swap(state["held"], turn))
                        state["held"] = jnp.concatenate([state["held"], got], 0)
                    if turn == rounds - 2:
                        state["last"] = swap(state["held"], rounds - 1)
                    return x
            else:
                state = {"kept": kept, "got": got, "step": rounds - 2, "message": message, "doubled": 0}

                def halve_on(x):
                    x, kept, got = together(x, state["kept"], state["got"])
                    state["kept"], state["got"] = halve(kept + got, state["step"])
                    state["step"] -= 1
                    return x

                def double_on(x):
                    x, got = together(x, swap(state["message"], state["doubled"]))
                    state["message"] = jnp.concatenate([state["message"], got], 0)
                    state["doubled"] += 1
                    return x

                def beside(x, turn):
                    if turn != 2 and state["doubled"] < rounds - 1:
                        x = double_on(x)
                    return halve_on(x) if turn % 2 and state["step"] > 0 else x

            w1, st1, *sums = begun
            w2, st2, packed, vc = start_part(owners[1], gene_row, size_row, u, p1, cb1, sums)
            mine, other = sum_gene(packed)
            mine = beside(mine, 0)
            hinv = beside(inverse_of(cells, mine, other), 1)
            for turn in range(2, FACTOR_STEPS + 1):
                mine, u = next_turn(block, size_row, u, mine, other, hinv, vc, w1, w2, st1, st2)
                mine, other = sum_gene(mine)
                if turn < FACTOR_STEPS:
                    mine = beside(mine, turn)
            if step < ITERS - 1:
                u, message, uc0, uc1 = step_update(block, u, mine, other, hinv, size_row, v, cb0, cb1)
            else:
                u = last_update(u, mine, other, hinv)
            if direct and step == ITERS - 1:
                if state["step"] >= 0:
                    mine = halve_on(mine)
                while state["doubled"] < rounds:
                    mine = double_on(mine)
                grad_v, traces = own_gradient(v, own_row, state["message"])
                traces = traces, *sum_gene(traces)
                while state["step"] >= 0:
                    grad_v = halve_on(grad_v)
            elif direct:
                for turn in range(FACTOR_STEPS, rounds - 1):
                    mine = beside(mine, turn)
            if direct and step < ITERS - 1:
                p0, p1 = state["held"], state["last"]
            elif direct:
                v = loadings_now(state["kept"], state["got"])
        return (u, v.reshape(rank, 1, width))

    return jax.shard_map(
        on_device,
        mesh=mesh,
        in_specs=(
            P("cell", "gene"),
            P("cell"),
            P("gene"),
            P(None, "cell"),
            P(None, "gene", "cell"),
        ),
        out_specs=(P(None, "cell"), P(None, "gene", "cell")),
        check_vma=False,
    )
```
